256 devices in a mesh: grp: 4 (over z_lo), gx: 8 (over y, z_hi), gy: 8 (over x, core).
Axes of the slice: x: 4, y: 4, z: 8 (z_hi: 2, z_lo: 4; z = z_hi * 4 + z_lo), core: 2. Of those that a mesh axis runs over, the one named last changes fastest.
Arguments:
- state: float32 [5, 32, 512, 1024], P(None, 'grp', 'gy', 'gx'), may hold values from -5 to 20, as said below
- tf_table: float32 [4, 4, 256], replicated, may hold values from 0 to 1
- owner: int32 [16, 1], replicated, may hold values from 0 to 3, as said below
- tf_index: int32 [16], replicated, may hold values from 0 to 3
- view_flip: int32 [512], P('gx'), may hold values 0 or 1
Outputs:
- new_state: float32 [5, 32, 512, 1024], P(None, 'grp', 'gy', 'gx')
- slot_image: float32 [32, 4, 512], P('grp', None, ('gx', 'gy'))
The draws below stay inside these ranges and needn't reach their ends.
Inputs may be any that keep to these rules, and one draw needn't show every extreme that they name: Each render owner is named by at most 8 bricks, and one by exactly 8. `state`: density in component 0 lies between 0.3 and 3, and the implied pressure is positive.
All inputs are finite; a program needn't handle non-finite values. No bound on the sum of `view_flip` on one device may be relied on, other than what follows from the above.
Results may differ from the reference program's by a relative error of at most 0.0003.
Values sent between devices are 32-bit elements; how exact they have to be, the bound alone decides.
No kernel may reach another device: no remote copies, remote signals or barrier semaphores. Data moves between devices by JAX's collectives and lax.ppermute only.
A program may use at most 128 MiB of HBM per device.

```python
import jax
import jax.numpy as jnp
from jax import lax

NT = 256
NTF = 4
NZ = 32
NY = 512
NX = 1024
NZC = 16
NYC = 256
NXC = 512
MOST = 8
SLOTS = 32
N_GRP = 4


def draw_state(key, part):
    key = jax.random.fold_in(key, 11)
    subkeys = jax.random.split(key, 3)
    grid_shape = (NZ, NY, NX)
    density = jax.random.uniform(subkeys[0], grid_shape, jnp.float32, 0.5, 2.0)
    speeds = jnp.clip(0.5 * jax.random.normal(subkeys[1], (3,) + grid_shape, jnp.float32), -1.4, 1.4)
    pressure = jax.random.uniform(subkeys[2], grid_shape, jnp.float32, 0.5, 2.0)
    energy = pressure / 0.4 + 0.5 * density * (speeds[0] * speeds[0] + speeds[1] * speeds[1] + speeds[2] * speeds[2])
    return jnp.concatenate([density[None], density[None] * speeds, energy[None]], 0)


def draw_owner(key, part):
    key = jax.random.fold_in(key, 23)
    subkeys = jax.random.split(key, 3)
    order = jax.random.permutation(subkeys[0], NZC)
    position = jnp.argsort(order, stable=True).astype(jnp.int32)
    busiest = jax.random.randint(subkeys[1], (), 0, N_GRP).astype(jnp.int32)
    others = (busiest + 1 + jax.random.randint(subkeys[2], (NZC,), 0, N_GRP - 1)) % N_GRP
    chosen = jnp.where(position < MOST, busiest, others.astype(jnp.int32))
    return chosen.astype(jnp.int32)[:, None]


def place_ends(drawn, key, least, top_value):
    dims = drawn.shape
    place = [jax.random.randint(jax.random.fold_in(key, axis), (), 0, dims[axis]) for axis in range(len(dims))]
    drawn = drawn.at[tuple(place)].set(least)
    longest = dims.index(max(dims))
    place[longest] = (place[longest] + 1) % dims[longest]
    return drawn.at[tuple(place)].set(top_value)


def setup_inputs(seed: int = 0) -> dict:
    arg_keys = jax.random.split(jax.random.key(seed), 6)
    state = draw_state(jax.random.fold_in(arg_keys[5], 71), 0)
    tf_table = jnp.clip(jax.random.uniform(arg_keys[1], (NTF, 4, NT), jnp.float32, 0.0, 1.0), 0.0, 1.0)
    owner = draw_owner(jax.random.fold_in(arg_keys[5], 71), 0)
    tf_index = place_ends(jax.random.randint(arg_keys[3], (NZC,), 0, NTF), jax.random.fold_in(arg_keys[3], 1), 0, NTF - 1).astype(jnp.int32)
    view_flip = place_ends((jax.random.randint(arg_keys[4], (NXC,), 0, 2) < 1).astype(jnp.int32), jax.random.fold_in(arg_keys[4], 1), 0, 1)
    return dict(state=state, tf_table=tf_table, owner=owner, tf_index=tf_index, view_flip=view_flip)


gamma_less = 0.4
step_size = 0.5
opacity_gain = 6.0
stencil_weights = (0.8, -0.2, 4.0 / 105.0, -1.0 / 280.0)

def primitives(state_slab):
    density = state_slab[0]
    east = state_slab[1] / density
    north = state_slab[2] / density
    upward = state_slab[3] / density
    pressure = gamma_less * (state_slab[4] - 0.5 * density * (east * east + north * north + upward * upward))
    return (density, east, north, upward, pressure)

def fluxes(state_slab, speeds, pressure, direction):
    normal_speed = speeds[direction]
    moment_flux = [state_slab[1 + c] * normal_speed for c in range(3)]
    moment_flux[direction] = moment_flux[direction] + pressure
    return jnp.stack([state_slab[0] * normal_speed] + moment_flux + [(state_slab[4] + pressure) * normal_speed])

def roll_stencil(values, along_dim):
    total = None
    for k in range(4):
        addend = stencil_weights[k] * (jnp.roll(values, -(k + 1), along_dim) - jnp.roll(values, k + 1, along_dim))
        total = addend if k == 0 else total + addend
    return total

def depth_stencil(values):
    total = None
    for k in range(4):
        addend = stencil_weights[k] * (values[5 + k] - values[3 - k])
        total = addend if k == 0 else total + addend
    return total

def plane_update(state_slab):
    middle = state_slab[:, 4]
    slab_parts = primitives(state_slab)
    middle_parts = tuple((p[4] for p in slab_parts))
    flux_east = fluxes(middle, middle_parts[1:4], middle_parts[4], 0)
    flux_north = fluxes(middle, middle_parts[1:4], middle_parts[4], 1)
    flux_up = fluxes(state_slab, slab_parts[1:4], slab_parts[4], 2)
    depth_term = depth_stencil(jnp.moveaxis(flux_up, 1, 0))
    change = roll_stencil(flux_east, -1) + roll_stencil(flux_north, -2) + depth_term
    updated = middle - step_size * change
    curl_first = roll_stencil(middle_parts[3], -2) - depth_stencil(slab_parts[2])
    curl_second = depth_stencil(slab_parts[1]) - roll_stencil(middle_parts[3], -1)
    curl_third = roll_stencil(middle_parts[2], -1) - roll_stencil(middle_parts[1], -2)
    spin = jnp.sqrt(curl_first * curl_first + curl_second * curl_second + curl_third * curl_third)
    return (updated, spin)

def plane_image(plane_density, plane_spin, table, flipped):
    grid_points = jnp.arange(NT).astype(table.dtype)

    def one_row(row_pair):
        density_row, spin_row = row_pair
        table_coord = (NT - 1) * jnp.clip((density_row - 0.9) / 0.6, 0.0, 1.0)
        weights = jnp.maximum(0.0, 1.0 - jnp.abs(table_coord[:, None] - grid_points[None, :]))
        entries = jnp.dot(table, weights.T, precision=lax.Precision.HIGHEST)
        opacity = opacity_gain * entries[3] * spin_row / (1.0 + spin_row) / NYC
        return (entries[:3] * opacity[None, :], opacity)
    colors, opacity = lax.map(one_row, (plane_density, plane_spin))
    survive = 1.0 - opacity
    forward = jnp.cumprod(survive, axis=0)
    front_reach = jnp.concatenate([jnp.ones_like(survive[:1]), forward[:-1]], 0)
    backward = jnp.flip(jnp.cumprod(jnp.flip(survive, 0), axis=0), 0)
    back_reach = jnp.concatenate([backward[1:], jnp.ones_like(survive[:1])], 0)
    reaching = jnp.where(flipped[None, :], back_reach, front_reach)
    radiance = lax.optimization_barrier(jnp.sum(reaching[:, None, :] * colors, axis=0))
    coverage = 1.0 - forward[-1]
    return jnp.concatenate([radiance, coverage[None]], 0)

def reference(state, tf_table, owner, tf_index, view_flip):
    wrapped = jnp.concatenate([state[:, -4:], state, state[:, :4]], axis=1)

    def one_plane(plane_index):
        state_slab = lax.dynamic_slice_in_dim(wrapped, plane_index, 9, 1)
        return plane_update(state_slab)
    updated, spin = lax.map(one_plane, jnp.arange(NZ).astype(jnp.int32))
    new_state = jnp.moveaxis(updated, 0, 1)
    coarse_density = state[0].reshape(NZC, 2, NYC, 2, NXC, 2).sum(axis=(1, 3, 5)) / 8.0
    coarse_spin = spin.reshape(NZC, 2, NYC, 2, NXC, 2).sum(axis=(1, 3, 5)) / 8.0
    flipped = view_flip == 1

    def one_brick(pack):
        return plane_image(pack[0], pack[1], tf_table[pack[2]], flipped)
    plane_rgba = lax.map(one_brick, (coarse_density, coarse_spin, tf_index))
    owners = owner[:, 0]
    earlier = jnp.arange(NZC)[:, None] > jnp.arange(NZC)[None, :]
    same_owner = owners[:, None] == owners[None, :]
    owner_rank = lax.optimization_barrier(jnp.sum(jnp.logical_and(earlier, same_owner).astype(jnp.int32), axis=1)).astype(jnp.int32)
    slot_index = (owners * MOST + owner_rank).astype(jnp.int32)
    slot_image = jnp.zeros((SLOTS, 4, NXC), plane_rgba.dtype).at[slot_index].set(plane_rgba)
    return (new_state, slot_image)
```

```python
import functools

import jax
import jax.numpy as jnp
import ml_dtypes
import numpy as np
from jax import lax
from jax.experimental import pallas as pl
from jax.experimental.pallas import tpu as pltpu
from jax.sharding import PartitionSpec as P

gamma_less = 0.4
step_size = 0.5
opacity_gain = 6.0
w1, w2, w3, w4 = (0.8, -0.2, 4.0 / 105.0, -1.0 / 280.0)
weights = (w1, w2, w3, w4)

f32 = jnp.float32
VM = pl.BlockSpec(memory_space=pltpu.VMEM)
SM = pl.BlockSpec(memory_space=pltpu.SMEM)


def weight(microseconds):
    return pl.CostEstimate(flops=int(microseconds * 1e9), bytes_accessed=1000000, transcendentals=0)


def params():
    return pltpu.CompilerParams(vmem_limit_bytes=24 * 2**20)


def turn(values, shift, axis):
    size = values.shape[axis]
    shift = shift % size
    return values if shift == 0 else pltpu.roll(values, shift, axis)


def primitives(rho, mx, my, mz, energy):
    inverse = 1.0 / rho
    u, v, w = mx * inverse, my * inverse, mz * inverse
    pressure = gamma_less * (energy - 0.5 * (mx * u + my * v + mz * w))
    return u, v, w, pressure


def east_fields(mx, my, mz, energy, u, v, w, p):
    return mx, mx * u + p, my * u, mz * u, (energy + p) * u, v, w


def north_fields(mx, my, mz, energy, u, v, w, p):
    return my, mx * v, my * v + p, mz * v, (energy + p) * v, u, w


def up_fields(mz, energy, u, v, w, p):
    return mz, mz * u, mz * v, mz * w + p, (energy + p) * w


def first_pack_kernel(state, low, high, y_low, y_high):
    for z in range(8):
        inverse = 1.0 / state[0, z]
        into = low if z < 4 else high
        into[0, z % 4] = state[1, z] * inverse
        into[1, z % 4] = state[2, z] * inverse
    sub = lax.broadcasted_iota(jnp.int32, (8, 128), 0)
    for c in range(5):
        for k in range(4):
            first, second = state[c, 2 * k, 0:8, :], state[c, 2 * k + 1, 0:8, :]
            y_low[c, k] = jnp.where(sub < 4, first, turn(second, 4, 0))
            first, second = state[c, 2 * k, 56:64, :], state[c, 2 * k + 1, 56:64, :]
            y_high[c, k] = jnp.where(sub < 4, turn(first, 4, 0), second)


def second_pack_kernel(state, x_low, x_high):
    lane = lax.broadcasted_iota(jnp.int32, (16, 128), 1)
    slot = lane >> 2
    for c in range(5):
        low = jnp.zeros((16, 128), f32)
        high = jnp.zeros((16, 128), f32)
        for j in range(32):
            row = j % 4 * 16
            moved = turn(state[c, j // 4, row : row + 16, :], 4 * j, 1)
            low = jnp.where(slot == j, moved, low)
            high = jnp.where(slot == (j - 1) % 32, moved, high)
        x_low[c] = low
        x_high[c] = high


def split(f):
    high = f.astype(jnp.bfloat16)
    low = (f - high.astype(f32)).astype(jnp.bfloat16)
    return high, low


def circulant_matrix():
    wide = np.zeros((128, 128), np.float32)
    for lane in range(128):
        for k in range(4):
            wide[(lane + k + 1) % 128, lane] += weights[k]
            wide[(lane - k - 1) % 128, lane] -= weights[k]
    high = wide.astype(ml_dtypes.bfloat16)
    low = (wide - high.astype(np.float32)).astype(ml_dtypes.bfloat16)
    row = np.concatenate([high, low], axis=1)
    return np.concatenate([row, row], axis=0)


def inner_kernel(state, from_south, from_north, matrix, partly, curls, yf, xf, dx):
    for ref, base in ((from_south, 4), (from_north, 72)):
        for k in range(4):
            rho, mx, my, mz, energy = (ref[c, k] for c in range(5))
            fields = north_fields(mx, my, mz, energy, *primitives(rho, mx, my, mz, energy))
            for n in range(7):
                yf[n, 2 * k, base : base + 4, :] = fields[n][0:4]
                yf[n, 2 * k + 1, base : base + 4, :] = fields[n][4:8]

    def plane(z, _):
        for r in range(0, 64, 16):
            rows = slice(r, r + 16)
            rho, mx, my, mz, energy = (state[c, z, rows, :] for c in range(5))
            parts = primitives(rho, mx, my, mz, energy)
            north = north_fields(mx, my, mz, energy, *parts)
            east = east_fields(mx, my, mz, energy, *parts)
            for n in range(7):
                yf[n, z, 8 + r : 24 + r, :] = north[n]
                high, low = split(east[n])
                xf[n, rows, 0:128] = high
                xf[n, rows, 128:256] = low
        for n in range(7):
            both = jnp.dot(xf[n], matrix[...], preferred_element_type=f32)
            dx[n] = both[:, 0:128] + both[:, 128:256]
        for r in range(0, 64, 16):
            rows = slice(r, r + 16)

            def along_y(n):
                total = None
                for k in range(4):
                    upper = yf[n, z, 9 + r + k : 25 + r + k, :]
                    lower = yf[n, z, 7 + r - k : 23 + r - k, :]
                    addend = weights[k] * (upper - lower)
                    total = addend if k == 0 else total + addend
                return total

            for c in range(5):
                partly[c, z, rows, :] = state[c, z, rows, :] - step_size * (dx[c, rows, :] + along_y(c))
            curls[0, z, rows, :] = along_y(6)
            curls[1, z, rows, :] = dx[6, rows, :]
            curls[2, z, rows, :] = dx[5, rows, :] - along_y(5)
        return 0

    lax.fori_loop(0, 8, plane, 0)


def edge_corrections(left_gap, right_gap):
    lane = lax.broadcasted_iota(jnp.int32, (16, 128), 1)
    place = lane & 3
    odd_slot = (lane >> 2 & 1) == 1
    left = jnp.zeros((16, 128), f32)
    right = jnp.zeros((16, 128), f32)
    for i in range(4):
        left += jnp.where(place + i <= 3, weights[3 - i], 0.0) * turn(left_gap, -i, 1)
        right += jnp.where(place >= i, weights[3 - i], 0.0) * turn(right_gap, i, 1)
    right = turn(right, -8, 1)
    return jnp.where(odd_slot, left, right), jnp.where(odd_slot, right, left)


def edge_tile(corrections, chunk):
    lane = lax.broadcasted_iota(jnp.int32, (16, 128), 1)
    fix = turn(corrections[chunk % 2], -4 * (chunk - 1), 1)
    return jnp.where(jnp.logical_or(lane < 4, lane >= 124), fix, 0.0)


def render_kernel(
    ray_total,
    pick,
    flip,
    density_of,
    curls,
    x_low,
    x_high,
    from_left,
    from_right,
    low_a,
    high_a,
    below_a,
    above_a,
    tables,
    segments,
    spins,
):
    def crossing(ref):
        inverse = 1.0 / ref[0]
        return ref[2] * inverse, ref[3] * inverse

    ours_low, ours_high, theirs_low, theirs_high = (
        crossing(r) for r in (x_low, x_high, from_left, from_right)
    )
    v_edge, w_edge = (
        edge_corrections(ours_high[n] - theirs_low[n], theirs_high[n] - ours_low[n]) for n in range(2)
    )
    blocks = (below_a, low_a, high_a, above_a)

    def depth(c, z, rows):
        total = None
        for k in range(4):
            up, down = z + 5 + k, z + 3 - k
            upper = blocks[up // 4][c, up % 4, rows, :]
            lower = blocks[down // 4][c, down % 4, rows, :]
            addend = weights[k] * (upper - lower)
            total = addend if k == 0 else total + addend
        return total

    for z in range(8):
        for b in range(4):
            rows = slice(16 * b, 16 * b + 16)
            chunk = 4 * z + b
            first = curls[0, z, rows, :] - depth(1, z, rows)
            second = depth(0, z, rows) - (curls[1, z, rows, :] + edge_tile(w_edge, chunk))
            third = curls[2, z, rows, :] + edge_tile(v_edge, chunk)
            spins[z, rows, :] = jnp.sqrt(first * first + second * second + third * third)

    flipped = flip[...] == 1
    for i in range(4):
        chosen = pick[i]
        halves = []
        for c in range(4):
            first = jnp.broadcast_to(tables[chosen, c : c + 1, 0:128], (8, 128))
            second = jnp.broadcast_to(tables[chosen, c : c + 1, 128:256], (8, 128))
            last = lax.broadcasted_iota(jnp.int32, (8, 128), 1) == 127
            after_first = jnp.where(last, turn(second, -1, 1), turn(first, -1, 1))
            after_second = jnp.where(last, second, turn(second, -1, 1))
            halves.append((first, second, after_first - first, after_second - second))

        total = None
        for m in range(4):

            def coarse(read):
                gathered = None
                for dz in range(2):
                    for dy in range(2):
                        part = read(2 * i + dz, pl.ds(2 * m + dy, 8, stride=8))
                        gathered = part if gathered is None else gathered + part
                return (gathered + turn(gathered, -1, 1)) * 0.125

            density = coarse(lambda z, rows: density_of[0, z, rows, :])
            spin = coarse(lambda z, rows: spins[z, rows, :])
            coord = 255.0 * jnp.clip((density - 0.9) / 0.6, 0.0, 1.0)
            cell = jnp.minimum(coord.astype(jnp.int32), 255)
            part = coord - cell.astype(f32)
            low_half = cell < 128
            index = cell & 127

            def look(a, b):
                return jnp.where(
                    low_half,
                    jnp.take_along_axis(a, index, axis=1),
                    jnp.take_along_axis(b, index, axis=1),
                )

            entries = [look(h[0], h[1]) + part * look(h[2], h[3]) for h in halves]
            opacity = opacity_gain * entries[3] * spin / (1.0 + spin) / ray_total
            piece = [entries[c] * opacity for c in range(3)] + [1.0 - opacity]
            total = piece if total is None else joined(total, piece, flipped)
        for span in (1, 2, 4):
            later = [turn(t, -span, 0) for t in total]
            total = joined(total, later, flipped)
        lanes = lax.broadcasted_iota(jnp.int32, (8, 128), 1)
        compact = (2 * lanes) & 127
        for c in range(4):
            row = jnp.take_along_axis(total[c], compact, axis=1)
            segments[4 * i + c : 4 * i + c + 1, :] = row[0:1, :]


def joined(near, far, flipped):
    colors = [
        jnp.where(flipped, far[c] + far[3] * near[c], near[c] + near[3] * far[c]) for c in range(3)
    ]
    return colors + [near[3] * far[3]]


def depth_kernel(partly, state, x_low, x_high, from_left, from_right, out, fz):
    def packed(ref):
        rho, mx, my, mz, energy = (ref[c] for c in range(5))
        return east_fields(mx, my, mz, energy, *primitives(rho, mx, my, mz, energy))[:5]

    ours_low, ours_high = packed(x_low), packed(x_high)
    theirs_low, theirs_high = packed(from_left), packed(from_right)
    edges = [
        edge_corrections(ours_high[n] - theirs_low[n], theirs_high[n] - ours_low[n]) for n in range(5)
    ]
    for z in range(8):
        for r in range(0, 64, 16):
            rows = slice(r, r + 16)
            rho, mx, my, mz, energy = (state[c, z, rows, :] for c in range(5))
            fields = up_fields(mz, energy, *primitives(rho, mx, my, mz, energy))
            for c in range(5):
                fz[c, z, rows, :] = fields[c]
    for c in range(5):
        for z in range(8):
            for b in range(4):
                rows = slice(16 * b, 16 * b + 16)
                total = edge_tile(edges[c], 4 * z + b)
                for k in range(4):
                    if z + k + 1 < 8:
                        total = total + weights[k] * fz[c, z + k + 1, rows, :]
                    if z - k - 1 >= 0:
                        total = total - weights[k] * fz[c, z - k - 1, rows, :]
                out[c, z, rows, :] = partly[c, z, rows, :] - step_size * total


def last_kernel(partly, below_a, below_b, above_a, above_b, out, fz):
    for side, (a, b) in enumerate(((below_a, below_b), (above_a, above_b))):
        for p in range(4):
            for r in range(0, 64, 16):
                rows = slice(r, r + 16)
                u, v = a[0, p, rows, :], a[1, p, rows, :]
                rho, mz, energy = b[0, p, rows, :], b[1, p, rows, :], b[2, p, rows, :]
                w = mz / rho
                pressure = gamma_less * (energy - 0.5 * (rho * (u * u + v * v) + mz * w))
                fields = up_fields(mz, energy, u, v, w, pressure)
                for c in range(5):
                    fz[c, 4 * side + p, rows, :] = step_size * fields[c]
    for c in range(5):
        for z in range(8):
            for r in range(0, 64, 16):
                rows = slice(r, r + 16)
                total = partly[c, z, rows, :]
                for k in range(4):
                    if z + k + 1 >= 8:
                        total = total - weights[k] * fz[c, 4 + z + k + 1 - 8, rows, :]
                    if z - k - 1 < 0:
                        total = total + weights[k] * fz[c, z - k - 1 + 4, rows, :]
                out[c, z, rows, :] = total


def compose_kernel(me, owner, flip, pieces, out):
    lane = lax.broadcasted_iota(jnp.int32, (4, 128), 1)
    channel = lane >> 3 & 3
    flipped = flip[...] == 1

    def passing(x):
        return jnp.where(
            channel == 3,
            x,
            jnp.where(
                channel == 2, turn(x, -8, 1), jnp.where(channel == 1, turn(x, -16, 1), turn(x, -24, 1))
            ),
        )

    total = pieces[:, 0, :]
    total_pass = passing(total)
    for j in range(1, 8):
        later = pieces[:, j, :]
        later_pass = passing(later)
        both = total_pass * later_pass
        color = jnp.where(flipped, later + later_pass * total, total + total_pass * later)
        total = jnp.where(channel == 3, both, color)
        total_pass = both
    total = jnp.where(channel == 3, 1.0 - total, total)
    sub = lax.broadcasted_iota(jnp.int32, (8, 128), 0)
    result = jnp.zeros((8, 128), f32)
    count = jnp.int32(0)
    shifted = [turn(total, -32 * i, 1) for i in range(4)]
    for b in range(16):
        mine = owner[b] == me[0]
        slot = jnp.where(mine, count, -1)
        count = jnp.where(mine, count + 1, count)
        row = jnp.broadcast_to(shifted[b % 4][b // 4 : b // 4 + 1, :], (8, 128))
        result = jnp.where(sub == slot, row, result)
    for c in range(4):
        out[:, c, :] = turn(result, -8 * c, 1)[:, 0:8]


def shape(*dims):
    return jax.ShapeDtypeStruct(dims, f32)


def ring(axis, step):
    count = lax.axis_size(axis)
    return [(i, (i + step) % count) for i in range(count)]


def after(value, *others):
    return lax.optimization_barrier((value, *others))[0]


def local(state, tf_table, owner, tf_index, view_flip):
    grp = lax.axis_index("grp")
    gy = lax.axis_index("gy")
    groups, depth = lax.axis_size("grp"), lax.axis_size("gy")
    low_a, high_a, y_low, y_high = pl.pallas_call(
        first_pack_kernel,
        out_shape=(shape(2, 4, 64, 128), shape(2, 4, 64, 128), shape(5, 4, 8, 128), shape(5, 4, 8, 128)),
        in_specs=[VM],
        out_specs=(VM, VM, VM, VM),
        compiler_params=params(),
    )(state)
    from_below_a = lax.ppermute(high_a, "grp", ring("grp", 1))
    from_above_a = lax.ppermute(low_a, "grp", ring("grp", -1))
    from_south = lax.ppermute(y_high, "gy", ring("gy", 1))
    from_north = lax.ppermute(y_low, "gy", ring("gy", -1))
    x_low, x_high = pl.pallas_call(
        second_pack_kernel,
        out_shape=(shape(5, 16, 128), shape(5, 16, 128)),
        in_specs=[VM],
        out_specs=(VM, VM),
        compiler_params=params(),
    )(after(state, y_low))
    from_left = lax.ppermute(x_high, "gx", ring("gx", 1))
    from_right = lax.ppermute(x_low, "gx", ring("gx", -1))
    partly, curls = pl.pallas_call(
        inner_kernel,
        out_shape=(shape(5, 8, 64, 128), shape(3, 8, 64, 128)),
        in_specs=[VM] * 4,
        out_specs=(VM, VM),
        scratch_shapes=[
            pltpu.VMEM((7, 8, 80, 128), f32),
            pltpu.VMEM((7, 64, 256), jnp.bfloat16),
            pltpu.VMEM((7, 64, 128), f32),
        ],
        compiler_params=params(),
        cost_estimate=weight(1),
    )(state, from_south, from_north, jnp.asarray(circulant_matrix()))

    late = after(state, from_above_a, from_below_a)
    from_above_b = lax.ppermute(jnp.stack([late[c, :4] for c in (0, 3, 4)]), "grp", ring("grp", -1))
    from_below_b = lax.ppermute(jnp.stack([late[c, 4:] for c in (0, 3, 4)]), "grp", ring("grp", 1))

    pick = lax.dynamic_slice_in_dim(tf_index, grp * 4, 4)
    flip = jnp.repeat(view_flip, 2)[None, :]
    segments = pl.pallas_call(
        functools.partial(render_kernel, float(depth * 32)),
        out_shape=shape(16, 128),
        in_specs=[SM] + [VM] * 12,
        out_specs=VM,
        scratch_shapes=[pltpu.VMEM((8, 64, 128), f32)],
        compiler_params=params(),
        cost_estimate=weight(60),
    )(
        pick, flip, state, curls, x_low, x_high, from_left, from_right,
        low_a, high_a, from_below_a, from_above_a, tf_table,
    )
    width = 64 // depth
    pieces = segments[:, :64].reshape(16, depth, width).transpose(1, 0, 2).reshape(depth, 16 * width)
    sent = jnp.tile(pieces, (groups, 1))
    received = lax.all_to_all(sent, ("grp", "gy"), 0, 0, tiled=True).reshape(groups, depth, 128)
    most = pl.pallas_call(
        depth_kernel,
        out_shape=shape(5, 8, 64, 128),
        in_specs=[VM] * 6,
        out_specs=VM,
        scratch_shapes=[pltpu.VMEM((5, 8, 64, 128), f32)],
        compiler_params=params(),
    )(after(partly, segments), state, x_low, x_high, from_left, from_right)
    new_state = pl.pallas_call(
        last_kernel,
        out_shape=shape(5, 8, 64, 128),
        in_specs=[VM] * 5,
        out_specs=VM,
        scratch_shapes=[pltpu.VMEM((5, 8, 64, 128), f32)],
        compiler_params=params(),
    )(most, from_below_a, from_below_b, from_above_a, from_above_b)
    own_flip = jnp.tile(lax.dynamic_slice_in_dim(view_flip, gy * width, width), 16)[None, :]
    image = pl.pallas_call(
        compose_kernel,
        out_shape=shape(8, 4, 8),
        in_specs=[SM, SM, VM, VM],
        out_specs=VM,
        compiler_params=params(),
    )(grp[None], owner[:, 0], own_flip, received)
    return (new_state, image)


def solution(mesh):
    placed = (P(None, "grp", "gy", "gx"), P(), P(), P(), P("gx"))
    return jax.shard_map(
        local,
        mesh=mesh,
        in_specs=placed,
        out_specs=(P(None, "grp", "gy", "gx"), P("grp", None, ("gx", "gy"))),
        check_vma=False,
    )
```

```python
import functools

import jax
import jax.numpy as jnp
from jax import lax
from jax.experimental import pallas as pl
from jax.experimental.pallas import tpu as pltpu
from jax.sharding import PartitionSpec as P

gamma_less = 0.4
step_size = 0.5
opacity_gain = 6.0
w1, w2, w3, w4 = (0.8, -0.2, 4.0 / 105.0, -1.0 / 280.0)
weights = (w1, w2, w3, w4)

f32 = jnp.float32
VM = pl.BlockSpec(memory_space=pltpu.VMEM)
SM = pl.BlockSpec(memory_space=pltpu.SMEM)
HB = pl.BlockSpec(memory_space=pltpu.HBM)


def weight(microseconds):
    return pl.CostEstimate(flops=int(microseconds * 1e9), bytes_accessed=1000000, transcendentals=0)


def params(mebibytes=2):
    return pltpu.CompilerParams(vmem_limit_bytes=mebibytes * 2**20)


def in_hbm(a):
    return pltpu.with_memory_space_constraint(a, pltpu.HBM)


def turn(values, shift, axis):
    size = values.shape[axis]
    shift = shift % size
    return values if shift == 0 else pltpu.roll(values, shift, axis)


def primitives(rho, mx, my, mz, energy):
    inverse = 1.0 / rho
    u, v, w = mx * inverse, my * inverse, mz * inverse
    pressure = gamma_less * (energy - 0.5 * (mx * u + my * v + mz * w))
    return u, v, w, pressure


def east_fields(mx, my, mz, energy, u, v, w, p):
    return mx, mx * u + p, my * u, mz * u, (energy + p) * u, v, w


def north_fields(mx, my, mz, energy, u, v, w, p):
    return my, mx * v, my * v + p, mz * v, (energy + p) * v, u, w


def up_fields(mz, energy, u, v, w, p):
    return mz, mz * u, mz * v, mz * w + p, (energy + p) * w


def first_pack_kernel(state, low, high, y_low, y_high):
    for z in range(8):
        inverse = 1.0 / state[0, z]
        into = low if z < 4 else high
        into[0, z % 4] = state[1, z] * inverse
        into[1, z % 4] = state[2, z] * inverse
    sub = lax.broadcasted_iota(jnp.int32, (8, 128), 0)
    for c in range(5):
        for k in range(4):
            first, second = state[c, 2 * k, 0:8, :], state[c, 2 * k + 1, 0:8, :]
            y_low[c, k] = jnp.where(sub < 4, first, turn(second, 4, 0))
            first, second = state[c, 2 * k, 56:64, :], state[c, 2 * k + 1, 56:64, :]
            y_high[c, k] = jnp.where(sub < 4, turn(first, 4, 0), second)


def second_pack_kernel(state, x_low, x_high):
    lane = lax.broadcasted_iota(jnp.int32, (16, 128), 1)
    slot = lane >> 2
    for c in range(5):
        low = jnp.zeros((16, 128), f32)
        high = jnp.zeros((16, 128), f32)
        for j in range(32):
            row = j % 4 * 16
            moved = turn(state[c, j // 4, row : row + 16, :], 4 * j, 1)
            low = jnp.where(slot == j, moved, low)
            high = jnp.where(slot == (j - 1) % 32, moved, high)
        x_low[c] = low
        x_high[c] = high


def third_pack_kernel(state, low_b, high_b):
    for n, c in enumerate((0, 3, 4)):
        low_b[n] = state[c, :4]
        high_b[n] = state[c, 4:]


def split(f):
    high = f.astype(jnp.bfloat16)
    low = (f - high.astype(f32)).astype(jnp.bfloat16)
    return high, low


def write_circulant(matrix):
    row = lax.broadcasted_iota(jnp.int32, (128, 128), 0)
    column = lax.broadcasted_iota(jnp.int32, (128, 128), 1)
    offset = (row - column) & 127
    wide = jnp.zeros((128, 128), f32)
    for k in range(4):
        wide = jnp.where(offset == k + 1, weights[k], wide)
        wide = jnp.where(offset == 127 - k, -weights[k], wide)
    high, low = split(wide)
    for half in (slice(0, 128), slice(128, 256)):
        matrix[half, 0:128] = high
        matrix[half, 128:256] = low


def inner_kernel(
    state, from_south, from_north, partly, curls, matrix, yf, xf, dx
):
    write_circulant(matrix)

    def fields_of(z, _):
        for r in range(0, 64, 16):
            rows = slice(r, r + 16)
            rho, mx, my, mz, energy = (state[c, z, rows, :] for c in range(5))
            parts = primitives(rho, mx, my, mz, energy)
            north_parts = north_fields(mx, my, mz, energy, *parts)
            east_parts = east_fields(mx, my, mz, energy, *parts)
            for n in range(7):
                yf[n, z, 8 + r : 24 + r, :] = north_parts[n]
                high, low = split(east_parts[n])
                xf[n, rows, 0:128] = high
                xf[n, rows, 128:256] = low
        for n in range(7):
            both = jnp.dot(xf[n], matrix[...], preferred_element_type=f32)
            dx[n, z] = both[:, 0:128] + both[:, 128:256]
        return 0

    lax.fori_loop(0, 8, fields_of, 0)
    for ref, base in ((from_south, 4), (from_north, 72)):
        for k in range(4):
            rho, mx, my, mz, energy = (ref[c, k] for c in range(5))
            fields = north_fields(mx, my, mz, energy, *primitives(rho, mx, my, mz, energy))
            for n in range(7):
                yf[n, 2 * k, base : base + 4, :] = fields[n][0:4]
                yf[n, 2 * k + 1, base : base + 4, :] = fields[n][4:8]

    def plane(z, _):
        for r in range(0, 64, 16):
            rows = slice(r, r + 16)

            def along_y(n):
                total = None
                for k in range(4):
                    upper = yf[n, z, 9 + r + k : 25 + r + k, :]
                    lower = yf[n, z, 7 + r - k : 23 + r - k, :]
                    addend = weights[k] * (upper - lower)
                    total = addend if k == 0 else total + addend
                return total

            for c in range(5):
                partly[c, z, rows, :] = state[c, z, rows, :] - step_size * (dx[c, z, rows, :] + along_y(c))
            curls[0, z, rows, :] = along_y(6)
            curls[1, z, rows, :] = dx[6, z, rows, :]
            curls[2, z, rows, :] = dx[5, z, rows, :] - along_y(5)
        return 0

    lax.fori_loop(0, 8, plane, 0)


def edge_corrections(left_gap, right_gap):
    lane = lax.broadcasted_iota(jnp.int32, (16, 128), 1)
    place = lane & 3
    odd_slot = (lane >> 2 & 1) == 1
    left = jnp.zeros((16, 128), f32)
    right = jnp.zeros((16, 128), f32)
    for i in range(4):
        left += jnp.where(place + i <= 3, weights[3 - i], 0.0) * turn(left_gap, -i, 1)
        right += jnp.where(place >= i, weights[3 - i], 0.0) * turn(right_gap, i, 1)
    right = turn(right, -8, 1)
    return jnp.where(odd_slot, left, right), jnp.where(odd_slot, right, left)


def edge_pairs(fields, x_low, x_high, from_left, from_right):
    refs = (x_low, x_high, from_left, from_right)
    return [
        edge_corrections(high - left, right - low)
        for low, high, left, right in zip(*[fields(lambda c, ref=ref: ref[c]) for ref in refs])
    ]


def edge_tile(corrections, chunk):
    lane = lax.broadcasted_iota(jnp.int32, (16, 128), 1)
    fix = turn(corrections[chunk % 2], -4 * (chunk - 1), 1)
    return jnp.where(jnp.logical_or(lane < 4, lane >= 124), fix, 0.0)


def render_kernel(
    ray_total,
    grp,
    index,
    flip,
    density_of,
    curls,
    x_low,
    x_high,
    from_left,
    from_right,
    below_a,
    above_a,
    tables,
    sent,
    spins,
    uv,
    sems,
):
    copies = [
        pltpu.make_async_copy(below_a, uv.at[:, 0:4], sems.at[0]),
        pltpu.make_async_copy(above_a, uv.at[:, 12:16], sems.at[1]),
    ]
    for copy in copies:
        copy.start()
    edges_of = (x_low, x_high, from_left, from_right)
    def own_plane(z, _):
        for r in range(0, 64, 16):
            rows = slice(r, r + 16)
            inverse = 1.0 / density_of[0, z, rows, :]
            uv[0, z + 4, rows, :] = density_of[1, z, rows, :] * inverse
            uv[1, z + 4, rows, :] = density_of[2, z, rows, :] * inverse
        return 0

    lax.fori_loop(0, 8, own_plane, 0)
    for copy in copies:
        copy.wait()

    def crossing(read):
        inverse = 1.0 / read(0)
        return read(2) * inverse, read(3) * inverse

    v_edge, w_edge = edge_pairs(crossing, *edges_of)
    def depth(c, z, rows):
        total = None
        for k in range(4):
            addend = weights[k] * (uv[c, z + 5 + k, rows, :] - uv[c, z + 3 - k, rows, :])
            total = addend if k == 0 else total + addend
        return total

    for z in range(8):
        for b in range(4):
            rows = slice(16 * b, 16 * b + 16)
            chunk = 4 * z + b
            first = curls[0, z, rows, :] - depth(1, z, rows)
            second = depth(0, z, rows) - (curls[1, z, rows, :] + edge_tile(w_edge, chunk))
            third = curls[2, z, rows, :] + edge_tile(v_edge, chunk)
            spins[z, rows, :] = jnp.sqrt(first * first + second * second + third * third)

    lanes = lax.broadcasted_iota(jnp.int32, (8, 128), 1)
    rows_of = lax.broadcasted_iota(jnp.int32, (8, 128), 0)
    piece_lane = 16 * rows_of + 2 * (lanes & 7)
    outgoing = jnp.zeros((8, 128), f32)
    flipped = spread_flip(flip, lanes >> 1) == 1
    for i in range(4):
        chosen = index[4 * grp[0] + i]
        halves = []
        for c in range(4):
            first = jnp.broadcast_to(tables[chosen, c : c + 1, 0:128], (8, 128))
            second = jnp.broadcast_to(tables[chosen, c : c + 1, 128:256], (8, 128))
            last = lax.broadcasted_iota(jnp.int32, (8, 128), 1) == 127
            after_first = jnp.where(last, turn(second, -1, 1), turn(first, -1, 1))
            after_second = jnp.where(last, second, turn(second, -1, 1))
            halves.append((first, second, after_first - first, after_second - second))

        total = None
        for m in range(4):

            def coarse(read):
                gathered = None
                for dz in range(2):
                    for dy in range(2):
                        part = read(2 * i + dz, pl.ds(2 * m + dy, 8, stride=8))
                        gathered = part if gathered is None else gathered + part
                return (gathered + turn(gathered, -1, 1)) * 0.125

            density = coarse(lambda z, rows: density_of[0, z, rows, :])
            spin = coarse(lambda z, rows: spins[z, rows, :])
            coord = 255.0 * jnp.clip((density - 0.9) / 0.6, 0.0, 1.0)
            cell = jnp.minimum(coord.astype(jnp.int32), 255)
            part = coord - cell.astype(f32)
            low_half = cell < 128
            entry = cell & 127

            def look(a, b):
                return jnp.where(
                    low_half,
                    jnp.take_along_axis(a, entry, axis=1),
                    jnp.take_along_axis(b, entry, axis=1),
                )

            entries = [look(h[0], h[1]) + part * look(h[2], h[3]) for h in halves]
            opacity = opacity_gain * entries[3] * spin / (1.0 + spin) / ray_total
            piece = [entries[c] * opacity for c in range(3)] + [1.0 - opacity]
            total = piece if total is None else joined(total, piece, flipped)
        for span in (1, 2, 4):
            later = [turn(t, -span, 0) for t in total]
            total = joined(total, later, flipped)
        for c in range(4):
            row = jnp.broadcast_to(total[c][0:1, :], (8, 128))
            row = jnp.take_along_axis(row, piece_lane, axis=1)
            outgoing = jnp.where(lanes >> 3 == 4 * i + c, row, outgoing)
    for g in range(4):
        sent[8 * g : 8 * g + 8, :] = outgoing


def spread_flip(flip, lane):
    both = jnp.concatenate([flip[...], flip[...]], axis=1)
    return jnp.take_along_axis(jnp.broadcast_to(both, lane.shape), lane, axis=1)


def joined(near, far, flipped):
    colors = [
        jnp.where(flipped, far[c] + far[3] * near[c], near[c] + near[3] * far[c]) for c in range(3)
    ]
    return colors + [near[3] * far[3]]


def depth_kernel(partly, state, *refs):
    edges_of, out, fz = refs[:4], refs[4], refs[5]
    for z in range(8):
        for r in range(0, 64, 16):
            rows = slice(r, r + 16)
            rho, mx, my, mz, energy = (state[c, z, rows, :] for c in range(5))
            fields = up_fields(mz, energy, *primitives(rho, mx, my, mz, energy))
            for c in range(5):
                fz[c, z, rows, :] = fields[c]

    def packed(read):
        rho, mx, my, mz, energy = (read(c) for c in range(5))
        return east_fields(mx, my, mz, energy, *primitives(rho, mx, my, mz, energy))[:5]

    edges = edge_pairs(packed, *edges_of)
    for c in range(5):
        for z in range(8):
            for b in range(4):
                rows = slice(16 * b, 16 * b + 16)
                total = edge_tile(edges[c], 4 * z + b)
                for k in range(4):
                    if z + k + 1 < 8:
                        total = total + weights[k] * fz[c, z + k + 1, rows, :]
                    if z - k - 1 >= 0:
                        total = total - weights[k] * fz[c, z - k - 1, rows, :]
                out[c, z, rows, :] = partly[c, z, rows, :] - step_size * total


def last_kernel(partly, *refs):
    below_in, below_b, above_in, above_b, out, fz, held, below_a, above_a, sems, out_sems = refs
    copies = [
        pltpu.make_async_copy(below_in, below_a, sems.at[0]),
        pltpu.make_async_copy(above_in, above_a, sems.at[1]),
    ]
    for copy in copies:
        copy.start()
    for copy in copies:
        copy.wait()

    def sending(c):
        return pltpu.make_async_copy(held.at[c], out.at[c], out_sems.at[c])

    for side, (a, b) in enumerate(((below_a, below_b), (above_a, above_b))):
        for p in range(4):
            for r in range(0, 64, 16):
                rows = slice(r, r + 16)
                u, v = a[0, p, rows, :], a[1, p, rows, :]
                rho, mz, energy = b[0, p, rows, :], b[1, p, rows, :], b[2, p, rows, :]
                w = mz / rho
                pressure = gamma_less * (energy - 0.5 * (rho * (u * u + v * v) + mz * w))
                fields = up_fields(mz, energy, u, v, w, pressure)
                for c in range(5):
                    fz[c, 4 * side + p, rows, :] = step_size * fields[c]
    for c in range(5):
        for z in range(8):
            for r in range(0, 64, 16):
                rows = slice(r, r + 16)
                total = partly[c, z, rows, :]
                for k in range(4):
                    if z + k + 1 >= 8:
                        total = total - weights[k] * fz[c, 4 + z + k + 1 - 8, rows, :]
                    if z - k - 1 < 0:
                        total = total + weights[k] * fz[c, z - k - 1 + 4, rows, :]
                held[c, z, rows, :] = total
        sending(c).start()
    for c in range(5):
        sending(c).wait()


def compose_kernel(me, depth, owner, flip, pieces, out):
    lane = lax.broadcasted_iota(jnp.int32, (4, 128), 1)
    channel = lane >> 3 & 3
    lanes = lax.broadcasted_iota(jnp.int32, (8, 128), 1)
    flipped = spread_flip(flip, 8 * depth[0] + (lanes & 7))[0:4] == 1

    def passing(x):
        return jnp.where(
            channel == 3,
            x,
            jnp.where(
                channel == 2, turn(x, -8, 1), jnp.where(channel == 1, turn(x, -16, 1), turn(x, -24, 1))
            ),
        )

    total = pieces[:, 0, :]
    total_pass = passing(total)
    for j in range(1, 8):
        later = pieces[:, j, :]
        later_pass = passing(later)
        both = total_pass * later_pass
        color = jnp.where(flipped, later + later_pass * total, total + total_pass * later)
        total = jnp.where(channel == 3, both, color)
        total_pass = both
    total = jnp.where(channel == 3, 1.0 - total, total)
    sub = lax.broadcasted_iota(jnp.int32, (8, 128), 0)
    result = jnp.zeros((8, 128), f32)
    count = jnp.int32(0)
    shifted = [turn(total, -32 * i, 1) for i in range(4)]
    for b in range(16):
        mine = owner[b] == me[0]
        slot = jnp.where(mine, count, -1)
        count = jnp.where(mine, count + 1, count)
        row = jnp.broadcast_to(shifted[b % 4][b // 4 : b // 4 + 1, :], (8, 128))
        result = jnp.where(sub == slot, row, result)
    for c in range(4):
        out[:, c, :] = turn(result, -8 * c, 1)[:, 0:8]


def shape(*dims):
    return jax.ShapeDtypeStruct(dims, f32)


def ring(axis, step):
    count = lax.axis_size(axis)
    return [(i, (i + step) % count) for i in range(count)]


def after(value, *others):
    return lax.optimization_barrier((value, *others))[0]


def local(state, tf_table, owner, tf_index, view_flip):
    grp = lax.axis_index("grp")
    gy = lax.axis_index("gy")
    groups, depth = lax.axis_size("grp"), lax.axis_size("gy")
    low_a, high_a, y_low, y_high = pl.pallas_call(
        first_pack_kernel,
        out_shape=(shape(2, 4, 64, 128), shape(2, 4, 64, 128), shape(5, 4, 8, 128), shape(5, 4, 8, 128)),
        in_specs=[VM],
        out_specs=(VM, VM, VM, VM),
        compiler_params=params(),
    )(state)
    from_below_a = lax.ppermute(high_a, "grp", ring("grp", 1))
    from_above_a = lax.ppermute(low_a, "grp", ring("grp", -1))
    from_south = lax.ppermute(y_high, "gy", ring("gy", 1))
    from_north = lax.ppermute(y_low, "gy", ring("gy", -1))
    x_low, x_high = pl.pallas_call(
        second_pack_kernel,
        out_shape=(shape(5, 16, 128), shape(5, 16, 128)),
        in_specs=[VM],
        out_specs=(VM, VM),
        compiler_params=params(),
    )(after(state, y_low))
    from_left = lax.ppermute(x_high, "gx", ring("gx", 1))
    from_right = lax.ppermute(x_low, "gx", ring("gx", -1))
    partly, curls = pl.pallas_call(
        inner_kernel,
        out_shape=(shape(5, 8, 64, 128), shape(3, 8, 64, 128)),
        in_specs=[VM, VM, VM],
        out_specs=(VM, VM),
        scratch_shapes=[
            pltpu.VMEM((256, 256), jnp.bfloat16),
            pltpu.VMEM((7, 8, 80, 128), f32),
            pltpu.VMEM((7, 64, 256), jnp.bfloat16),
            pltpu.VMEM((7, 8, 64, 128), f32),
        ],
        compiler_params=params(12),
        cost_estimate=weight(0.3),
    )(state, from_south, from_north)

    low_b, high_b = pl.pallas_call(
        third_pack_kernel,
        out_shape=(shape(3, 4, 64, 128), shape(3, 4, 64, 128)),
        in_specs=[VM],
        out_specs=(VM, VM),
        compiler_params=params(),
        cost_estimate=weight(0.3),
    )(after(state, x_low))
    low_b, high_b = lax.optimization_barrier((low_b, high_b, from_above_a, from_below_a))[:2]
    from_above_b = lax.ppermute(low_b, "grp", ring("grp", -1))
    from_below_b = lax.ppermute(high_b, "grp", ring("grp", 1))

    flip = view_flip[None, :]
    sent = pl.pallas_call(
        functools.partial(render_kernel, float(depth * 32)),
        out_shape=shape(32, 128),
        in_specs=[SM] * 2 + [VM] * 7 + [HB] * 2 + [VM],
        out_specs=VM,
        scratch_shapes=[
            pltpu.VMEM((8, 64, 128), f32),
            pltpu.VMEM((2, 16, 64, 128), f32),
            pltpu.SemaphoreType.DMA((2,)),
        ],
        compiler_params=params(4),
        cost_estimate=weight(60),
    )(
        grp[None], tf_index, flip, state, curls,
        x_low, x_high, from_left, from_right, in_hbm(from_below_a), in_hbm(from_above_a), tf_table,
    )
    received = lax.all_to_all(sent, ("grp", "gy"), 0, 0, tiled=True).reshape(groups, depth, 128)
    most = pl.pallas_call(
        depth_kernel,
        out_shape=shape(5, 8, 64, 128),
        in_specs=[VM] * 6,
        out_specs=VM,
        scratch_shapes=[pltpu.VMEM((5, 8, 64, 128), f32)],
        compiler_params=params(6),
    )(after(partly, sent), state, x_low, x_high, from_left, from_right)
    new_state = pl.pallas_call(
        last_kernel,
        out_shape=shape(5, 8, 64, 128),
        in_specs=[VM, HB, VM, HB, VM],
        out_specs=HB,
        scratch_shapes=[
            pltpu.VMEM((5, 8, 64, 128), f32),
            pltpu.VMEM((5, 8, 64, 128), f32),
            pltpu.VMEM((2, 4, 64, 128), f32),
            pltpu.VMEM((2, 4, 64, 128), f32),
            pltpu.SemaphoreType.DMA((2,)),
            pltpu.SemaphoreType.DMA((5,)),
        ],
        compiler_params=params(6),
    )(most, in_hbm(from_below_a), from_below_b, in_hbm(from_above_a), from_above_b)
    image = pl.pallas_call(
        compose_kernel,
        out_shape=shape(8, 4, 8),
        in_specs=[SM, SM, SM, VM, VM],
        out_specs=VM,
        compiler_params=params(),
    )(grp[None], gy[None], owner[:, 0], flip, after(received, new_state))
    return (new_state, image)


def solution(mesh):
    placed = (P(None, "grp", "gy", "gx"), P(), P(), P(), P("gx"))
    return jax.shard_map(
        local,
        mesh=mesh,
        in_specs=placed,
        out_specs=(P(None, "grp", "gy", "gx"), P("grp", None, ("gx", "gy"))),
        check_vma=False,
    )
```

```python
import functools

import jax
import jax.numpy as jnp
from jax import lax
from jax.experimental import pallas as pl
from jax.experimental.pallas import tpu as pltpu
from jax.sharding import PartitionSpec as P

gamma_less = 0.4
step_size = 0.5
opacity_gain = 6.0
w1, w2, w3, w4 = (0.8, -0.2, 4.0 / 105.0, -1.0 / 280.0)
weights = (w1, w2, w3, w4)

f32 = jnp.float32
VM = pl.BlockSpec(memory_space=pltpu.VMEM)
SM = pl.BlockSpec(memory_space=pltpu.SMEM)
HB = pl.BlockSpec(memory_space=pltpu.HBM)


def weight(microseconds):
    return pl.CostEstimate(flops=int(microseconds * 1e9), bytes_accessed=1000000, transcendentals=0)


def params(mebibytes=2):
    return pltpu.CompilerParams(vmem_limit_bytes=mebibytes * 2**20)


def in_hbm(a):
    return pltpu.with_memory_space_constraint(a, pltpu.HBM)


def turn(values, shift, axis):
    size = values.shape[axis]
    shift = shift % size
    return values if shift == 0 else pltpu.roll(values, shift, axis)


def primitives(rho, mx, my, mz, energy):
    inverse = 1.0 / rho
    u, v, w = mx * inverse, my * inverse, mz * inverse
    pressure = gamma_less * (energy - 0.5 * (mx * u + my * v + mz * w))
    return u, v, w, pressure


def east_fields(mx, my, mz, energy, u, v, w, p):
    return mx, mx * u + p, my * u, mz * u, (energy + p) * u, v, w


def north_fields(mx, my, mz, energy, u, v, w, p):
    return my, mx * v, my * v + p, mz * v, (energy + p) * v, u, w


def up_fields(mz, energy, u, v, w, p):
    return mz, mz * u, mz * v, mz * w + p, (energy + p) * w


def first_pack_kernel(state, low, high, y_low, y_high):
    for z in range(8):
        inverse = 1.0 / state[0, z]
        into = low if z < 4 else high
        into[0, z % 4] = state[1, z] * inverse
        into[1, z % 4] = state[2, z] * inverse
    sub = lax.broadcasted_iota(jnp.int32, (8, 128), 0)
    for c in range(5):
        for k in range(4):
            first, second = state[c, 2 * k, 0:8, :], state[c, 2 * k + 1, 0:8, :]
            y_low[c, k] = jnp.where(sub < 4, first, turn(second, 4, 0))
            first, second = state[c, 2 * k, 56:64, :], state[c, 2 * k + 1, 56:64, :]
            y_high[c, k] = jnp.where(sub < 4, turn(first, 4, 0), second)


def second_pack_kernel(state, x_low, x_high):
    lane = lax.broadcasted_iota(jnp.int32, (16, 128), 1)
    slot = lane >> 2
    for c in range(5):
        low = jnp.zeros((16, 128), f32)
        high = jnp.zeros((16, 128), f32)
        for j in range(32):
            row = j % 4 * 16
            moved = turn(state[c, j // 4, row : row + 16, :], 4 * j, 1)
            low = jnp.where(slot == j, moved, low)
            high = jnp.where(slot == (j - 1) % 32, moved, high)
        x_low[c] = low
        x_high[c] = high


def third_pack_kernel(state, low_b, high_b):
    for n, c in enumerate((0, 3, 4)):
        low_b[n] = state[c, :4]
        high_b[n] = state[c, 4:]


def split(f):
    high = f.astype(jnp.bfloat16)
    low = (f - high.astype(f32)).astype(jnp.bfloat16)
    return high, low


def write_circulant(matrix):
    row = lax.broadcasted_iota(jnp.int32, (128, 128), 0)
    column = lax.broadcasted_iota(jnp.int32, (128, 128), 1)
    offset = (row - column) & 127
    wide = jnp.zeros((128, 128), f32)
    for k in range(4):
        wide = jnp.where(offset == k + 1, weights[k], wide)
        wide = jnp.where(offset == 127 - k, -weights[k], wide)
    high, low = split(wide)
    for half in (slice(0, 128), slice(128, 256)):
        matrix[half, 0:128] = high
        matrix[half, 128:256] = low


def inner_kernel(state, from_south, from_north, partly, curls, matrix, yf, xf, dx):
    write_circulant(matrix)
    for ref, base in ((from_south, 4), (from_north, 72)):
        for k in range(4):
            rho, mx, my, mz, energy = (ref[c, k] for c in range(5))
            fields = north_fields(mx, my, mz, energy, *primitives(rho, mx, my, mz, energy))
            for n in range(7):
                yf[n, 2 * k, base : base + 4, :] = fields[n][0:4]
                yf[n, 2 * k + 1, base : base + 4, :] = fields[n][4:8]

    def plane(z, _):
        for r in range(0, 64, 16):
            rows = slice(r, r + 16)
            rho, mx, my, mz, energy = (state[c, z, rows, :] for c in range(5))
            parts = primitives(rho, mx, my, mz, energy)
            north = north_fields(mx, my, mz, energy, *parts)
            east = east_fields(mx, my, mz, energy, *parts)
            for n in range(7):
                yf[n, z, 8 + r : 24 + r, :] = north[n]
                high, low = split(east[n])
                xf[n, rows, 0:128] = high
                xf[n, rows, 128:256] = low
        for n in range(7):
            both = jnp.dot(xf[n], matrix[...], preferred_element_type=f32)
            dx[n] = both[:, 0:128] + both[:, 128:256]
        for r in range(0, 64, 16):
            rows = slice(r, r + 16)

            def along_y(n):
                total = None
                for k in range(4):
                    upper = yf[n, z, 9 + r + k : 25 + r + k, :]
                    lower = yf[n, z, 7 + r - k : 23 + r - k, :]
                    addend = weights[k] * (upper - lower)
                    total = addend if k == 0 else total + addend
                return total

            for c in range(5):
                partly[c, z, rows, :] = state[c, z, rows, :] - step_size * (dx[c, rows, :] + along_y(c))
            curls[0, z, rows, :] = along_y(6)
            curls[1, z, rows, :] = dx[6, rows, :]
            curls[2, z, rows, :] = dx[5, rows, :] - along_y(5)
        return 0

    lax.fori_loop(0, 8, plane, 0)


def edge_corrections(left_gap, right_gap):
    lane = lax.broadcasted_iota(jnp.int32, (16, 128), 1)
    place = lane & 3
    odd_slot = (lane >> 2 & 1) == 1
    left = jnp.zeros((16, 128), f32)
    right = jnp.zeros((16, 128), f32)
    for i in range(4):
        left += jnp.where(place + i <= 3, weights[3 - i], 0.0) * turn(left_gap, -i, 1)
        right += jnp.where(place >= i, weights[3 - i], 0.0) * turn(right_gap, i, 1)
    right = turn(right, -8, 1)
    return jnp.where(odd_slot, left, right), jnp.where(odd_slot, right, left)


def edge_pairs(fields, x_low, x_high, from_left, from_right):
    refs = (x_low, x_high, from_left, from_right)
    return [
        edge_corrections(high - left, right - low)
        for low, high, left, right in zip(*[fields(lambda c, ref=ref: ref[c]) for ref in refs])
    ]


def edge_tile(corrections, chunk):
    lane = lax.broadcasted_iota(jnp.int32, (16, 128), 1)
    fix = turn(corrections[chunk % 2], -4 * (chunk - 1), 1)
    return jnp.where(jnp.logical_or(lane < 4, lane >= 124), fix, 0.0)


def render_kernel(
    ray_total,
    grp,
    index,
    flip,
    density_of,
    curls,
    x_low,
    x_high,
    left_in,
    right_in,
    below_a,
    above_a,
    tables,
    sent,
    spins,
    uv,
    looked,
    from_left,
    from_right,
    sems,
):
    copies = [
        pltpu.make_async_copy(below_a, uv.at[:, 0:4], sems.at[0]),
        pltpu.make_async_copy(above_a, uv.at[:, 12:16], sems.at[1]),
        pltpu.make_async_copy(left_in, from_left, sems.at[2]),
        pltpu.make_async_copy(right_in, from_right, sems.at[3]),
    ]
    for copy in copies:
        copy.start()
    edges_of = (x_low, x_high, from_left, from_right)
    def own_plane(z, _):
        for r in range(0, 64, 16):
            rows = slice(r, r + 16)
            inverse = 1.0 / density_of[0, z, rows, :]
            uv[0, z + 4, rows, :] = density_of[1, z, rows, :] * inverse
            uv[1, z + 4, rows, :] = density_of[2, z, rows, :] * inverse
        return 0

    lax.fori_loop(0, 8, own_plane, 0)

    def coarse(read, i, m):
        gathered = None
        for dz in range(2):
            for dy in range(2):
                part = read(2 * i + dz, pl.ds(2 * m + dy, 8, stride=8))
                gathered = part if gathered is None else gathered + part
        return (gathered + turn(gathered, -1, 1)) * 0.125

    for i in range(4):
        chosen = index[4 * grp[0] + i]
        halves = []
        for c in range(4):
            first = jnp.broadcast_to(tables[chosen, c : c + 1, 0:128], (8, 128))
            second = jnp.broadcast_to(tables[chosen, c : c + 1, 128:256], (8, 128))
            last = lax.broadcasted_iota(jnp.int32, (8, 128), 1) == 127
            after_first = jnp.where(last, turn(second, -1, 1), turn(first, -1, 1))
            after_second = jnp.where(last, second, turn(second, -1, 1))
            halves.append((first, second, after_first - first, after_second - second))
        for m in range(4):
            density = coarse(lambda z, rows: density_of[0, z, rows, :], i, m)
            coord = 255.0 * jnp.clip((density - 0.9) / 0.6, 0.0, 1.0)
            cell = jnp.minimum(coord.astype(jnp.int32), 255)
            part = coord - cell.astype(f32)
            low_half = cell < 128
            entry = cell & 127

            def look(a, b):
                return jnp.where(
                    low_half,
                    jnp.take_along_axis(a, entry, axis=1),
                    jnp.take_along_axis(b, entry, axis=1),
                )

            for c, h in enumerate(halves):
                looked[i, m, c] = look(h[0], h[1]) + part * look(h[2], h[3])

    for copy in copies[2:]:
        copy.wait()

    def crossing(read):
        inverse = 1.0 / read(0)
        return read(2) * inverse, read(3) * inverse

    v_edge, w_edge = edge_pairs(crossing, *edges_of)
    for copy in copies[:2]:
        copy.wait()

    def depth(c, z, rows):
        total = None
        for k in range(4):
            addend = weights[k] * (uv[c, z + 5 + k, rows, :] - uv[c, z + 3 - k, rows, :])
            total = addend if k == 0 else total + addend
        return total

    for z in range(8):
        for b in range(4):
            rows = slice(16 * b, 16 * b + 16)
            chunk = 4 * z + b
            first = curls[0, z, rows, :] - depth(1, z, rows)
            second = depth(0, z, rows) - (curls[1, z, rows, :] + edge_tile(w_edge, chunk))
            third = curls[2, z, rows, :] + edge_tile(v_edge, chunk)
            spins[z, rows, :] = jnp.sqrt(first * first + second * second + third * third)

    lanes = lax.broadcasted_iota(jnp.int32, (8, 128), 1)
    rows_of = lax.broadcasted_iota(jnp.int32, (8, 128), 0)
    piece_lane = 16 * rows_of + 2 * (lanes & 7)
    outgoing = jnp.zeros((8, 128), f32)
    flipped = spread_flip(flip, lanes >> 1) == 1
    for i in range(4):
        total = None
        for m in range(4):
            spin = coarse(lambda z, rows: spins[z, rows, :], i, m)
            entries = [looked[i, m, c] for c in range(4)]
            opacity = opacity_gain * entries[3] * spin / (1.0 + spin) / ray_total
            piece = [entries[c] * opacity for c in range(3)] + [1.0 - opacity]
            total = piece if total is None else joined(total, piece, flipped)
        for span in (1, 2, 4):
            later = [turn(t, -span, 0) for t in total]
            total = joined(total, later, flipped)
        for c in range(4):
            row = jnp.broadcast_to(total[c][0:1, :], (8, 128))
            row = jnp.take_along_axis(row, piece_lane, axis=1)
            outgoing = jnp.where(lanes >> 3 == 4 * i + c, row, outgoing)
    for g in range(4):
        sent[8 * g : 8 * g + 8, :] = outgoing


def spread_flip(flip, lane):
    both = jnp.concatenate([flip[...], flip[...]], axis=1)
    return jnp.take_along_axis(jnp.broadcast_to(both, lane.shape), lane, axis=1)


def joined(near, far, flipped):
    colors = [
        jnp.where(flipped, far[c] + far[3] * near[c], near[c] + near[3] * far[c]) for c in range(3)
    ]
    return colors + [near[3] * far[3]]


def depth_kernel(partly, state, *refs):
    edges_of, out, fz = refs[:4], refs[4], refs[5]
    for z in range(8):
        for r in range(0, 64, 16):
            rows = slice(r, r + 16)
            rho, mx, my, mz, energy = (state[c, z, rows, :] for c in range(5))
            fields = up_fields(mz, energy, *primitives(rho, mx, my, mz, energy))
            for c in range(5):
                fz[c, z, rows, :] = fields[c]

    def packed(read):
        rho, mx, my, mz, energy = (read(c) for c in range(5))
        return east_fields(mx, my, mz, energy, *primitives(rho, mx, my, mz, energy))[:5]

    edges = edge_pairs(packed, *edges_of)
    for c in range(5):
        for z in range(8):
            for b in range(4):
                rows = slice(16 * b, 16 * b + 16)
                total = edge_tile(edges[c], 4 * z + b)
                for k in range(4):
                    if z + k + 1 < 8:
                        total = total + weights[k] * fz[c, z + k + 1, rows, :]
                    if z - k - 1 >= 0:
                        total = total - weights[k] * fz[c, z - k - 1, rows, :]
                out[c, z, rows, :] = partly[c, z, rows, :] - step_size * total


def last_kernel(partly, *refs):
    below_in, below_b, above_in, above_b, out, fz, held, below_a, above_a, sems, out_sems = refs
    copies = [
        pltpu.make_async_copy(below_in, below_a, sems.at[0]),
        pltpu.make_async_copy(above_in, above_a, sems.at[1]),
    ]
    for copy in copies:
        copy.start()
    for copy in copies:
        copy.wait()

    def sending(c):
        return pltpu.make_async_copy(held.at[c], out.at[c], out_sems.at[c])

    for side, (a, b) in enumerate(((below_a, below_b), (above_a, above_b))):
        for p in range(4):
            for r in range(0, 64, 16):
                rows = slice(r, r + 16)
                u, v = a[0, p, rows, :], a[1, p, rows, :]
                rho, mz, energy = b[0, p, rows, :], b[1, p, rows, :], b[2, p, rows, :]
                w = mz / rho
                pressure = gamma_less * (energy - 0.5 * (rho * (u * u + v * v) + mz * w))
                fields = up_fields(mz, energy, u, v, w, pressure)
                for c in range(5):
                    fz[c, 4 * side + p, rows, :] = step_size * fields[c]
    for c in range(5):
        for z in range(8):
            for r in range(0, 64, 16):
                rows = slice(r, r + 16)
                total = partly[c, z, rows, :]
                for k in range(4):
                    if z + k + 1 >= 8:
                        total = total - weights[k] * fz[c, 4 + z + k + 1 - 8, rows, :]
                    if z - k - 1 < 0:
                        total = total + weights[k] * fz[c, z - k - 1 + 4, rows, :]
                held[c, z, rows, :] = total
        sending(c).start()
    for c in range(5):
        sending(c).wait()


def compose_kernel(me, depth, owner, flip, pieces, out):
    lane = lax.broadcasted_iota(jnp.int32, (4, 128), 1)
    channel = lane >> 3 & 3
    lanes = lax.broadcasted_iota(jnp.int32, (8, 128), 1)
    flipped = spread_flip(flip, 8 * depth[0] + (lanes & 7))[0:4] == 1

    def passing(x):
        return jnp.where(
            channel == 3,
            x,
            jnp.where(
                channel == 2, turn(x, -8, 1), jnp.where(channel == 1, turn(x, -16, 1), turn(x, -24, 1))
            ),
        )

    total = pieces[:, 0, :]
    total_pass = passing(total)
    for j in range(1, 8):
        later = pieces[:, j, :]
        later_pass = passing(later)
        both = total_pass * later_pass
        color = jnp.where(flipped, later + later_pass * total, total + total_pass * later)
        total = jnp.where(channel == 3, both, color)
        total_pass = both
    total = jnp.where(channel == 3, 1.0 - total, total)
    sub = lax.broadcasted_iota(jnp.int32, (8, 128), 0)
    result = jnp.zeros((8, 128), f32)
    count = jnp.int32(0)
    shifted = [turn(total, -32 * i, 1) for i in range(4)]
    for b in range(16):
        mine = owner[b] == me[0]
        slot = jnp.where(mine, count, -1)
        count = jnp.where(mine, count + 1, count)
        row = jnp.broadcast_to(shifted[b % 4][b // 4 : b // 4 + 1, :], (8, 128))
        result = jnp.where(sub == slot, row, result)
    for c in range(4):
        out[:, c, :] = turn(result, -8 * c, 1)[:, 0:8]


def shape(*dims):
    return jax.ShapeDtypeStruct(dims, f32)


def ring(axis, step):
    count = lax.axis_size(axis)
    return [(i, (i + step) % count) for i in range(count)]


def after(value, *others):
    return lax.optimization_barrier((value, *others))[0]


def local(state, tf_table, owner, tf_index, view_flip):
    grp = lax.axis_index("grp")
    gy = lax.axis_index("gy")
    groups, depth = lax.axis_size("grp"), lax.axis_size("gy")
    low_a, high_a, y_low, y_high = pl.pallas_call(
        first_pack_kernel,
        out_shape=(shape(2, 4, 64, 128), shape(2, 4, 64, 128), shape(5, 4, 8, 128), shape(5, 4, 8, 128)),
        in_specs=[VM],
        out_specs=(VM, VM, VM, VM),
        compiler_params=params(),
    )(state)
    from_below_a = lax.ppermute(high_a, "grp", ring("grp", 1))
    from_above_a = lax.ppermute(low_a, "grp", ring("grp", -1))
    from_south = lax.ppermute(y_high, "gy", ring("gy", 1))
    from_north = lax.ppermute(y_low, "gy", ring("gy", -1))
    x_low, x_high = pl.pallas_call(
        second_pack_kernel,
        out_shape=(shape(5, 16, 128), shape(5, 16, 128)),
        in_specs=[VM],
        out_specs=(VM, VM),
        compiler_params=params(),
    )(after(state, y_low))
    from_left = lax.ppermute(x_high, "gx", ring("gx", 1))
    from_right = lax.ppermute(x_low, "gx", ring("gx", -1))
    partly, curls = pl.pallas_call(
        inner_kernel,
        out_shape=(shape(5, 8, 64, 128), shape(3, 8, 64, 128)),
        in_specs=[VM, VM, VM],
        out_specs=(VM, VM),
        scratch_shapes=[
            pltpu.VMEM((256, 256), jnp.bfloat16),
            pltpu.VMEM((7, 8, 80, 128), f32),
            pltpu.VMEM((7, 64, 256), jnp.bfloat16),
            pltpu.VMEM((7, 64, 128), f32),
        ],
        compiler_params=params(12),
        cost_estimate=weight(0.3),
    )(state, from_south, from_north)

    low_b, high_b = pl.pallas_call(
        third_pack_kernel,
        out_shape=(shape(3, 4, 64, 128), shape(3, 4, 64, 128)),
        in_specs=[VM],
        out_specs=(VM, VM),
        compiler_params=params(),
        cost_estimate=weight(0.3),
    )(after(state, x_low))
    low_b, high_b = lax.optimization_barrier((low_b, high_b, from_above_a, from_below_a))[:2]
    from_above_b = lax.ppermute(low_b, "grp", ring("grp", -1))
    from_below_b = lax.ppermute(high_b, "grp", ring("grp", 1))

    flip = view_flip[None, :]
    sent = pl.pallas_call(
        functools.partial(render_kernel, float(depth * 32)),
        out_shape=shape(32, 128),
        in_specs=[SM] * 2 + [VM] * 5 + [HB] * 4 + [VM],
        out_specs=VM,
        scratch_shapes=[
            pltpu.VMEM((8, 64, 128), f32),
            pltpu.VMEM((2, 16, 64, 128), f32),
            pltpu.VMEM((4, 4, 4, 8, 128), f32),
            pltpu.VMEM((5, 16, 128), f32),
            pltpu.VMEM((5, 16, 128), f32),
            pltpu.SemaphoreType.DMA((4,)),
        ],
        compiler_params=params(4),
        cost_estimate=weight(60),
    )(
        grp[None], tf_index, flip, state, curls,
        x_low, x_high, from_left, from_right, in_hbm(from_below_a), in_hbm(from_above_a), tf_table,
    )
    received = lax.all_to_all(sent, ("grp", "gy"), 0, 0, tiled=True).reshape(groups, depth, 128)
    most = pl.pallas_call(
        depth_kernel,
        out_shape=shape(5, 8, 64, 128),
        in_specs=[VM] * 6,
        out_specs=VM,
        scratch_shapes=[pltpu.VMEM((5, 8, 64, 128), f32)],
        compiler_params=params(6),
    )(after(partly, sent), state, x_low, x_high, from_left, from_right)
    new_state = pl.pallas_call(
        last_kernel,
        out_shape=shape(5, 8, 64, 128),
        in_specs=[VM, HB, VM, HB, VM],
        out_specs=HB,
        scratch_shapes=[
            pltpu.VMEM((5, 8, 64, 128), f32),
            pltpu.VMEM((5, 8, 64, 128), f32),
            pltpu.VMEM((2, 4, 64, 128), f32),
            pltpu.VMEM((2, 4, 64, 128), f32),
            pltpu.SemaphoreType.DMA((2,)),
            pltpu.SemaphoreType.DMA((5,)),
        ],
        compiler_params=params(6),
    )(most, in_hbm(from_below_a), from_below_b, in_hbm(from_above_a), from_above_b)
    image = pl.pallas_call(
        compose_kernel,
        out_shape=shape(8, 4, 8),
        in_specs=[SM, SM, SM, VM, VM],
        out_specs=VM,
        compiler_params=params(),
    )(grp[None], gy[None], owner[:, 0], flip, after(received, new_state))
    return (new_state, image)


def solution(mesh):
    placed = (P(None, "grp", "gy", "gx"), P(), P(), P(), P("gx"))
    return jax.shard_map(
        local,
        mesh=mesh,
        in_specs=placed,
        out_specs=(P(None, "grp", "gy", "gx"), P("grp", None, ("gx", "gy"))),
        check_vma=False,
    )
```

```python
import functools

import jax
import jax.numpy as jnp
from jax import lax
from jax.experimental import pallas as pl
from jax.experimental.pallas import tpu as pltpu
from jax.sharding import PartitionSpec as P

gamma_less = 0.4
step_size = 0.5
opacity_gain = 6.0
w1, w2, w3, w4 = (0.8, -0.2, 4.0 / 105.0, -1.0 / 280.0)
weights = (w1, w2, w3, w4)

f32 = jnp.float32
VM = pl.BlockSpec(memory_space=pltpu.VMEM)
SM = pl.BlockSpec(memory_space=pltpu.SMEM)
HB = pl.BlockSpec(memory_space=pltpu.HBM)


def weight(microseconds):
    return pl.CostEstimate(flops=int(microseconds * 1e9), bytes_accessed=1000000, transcendentals=0)


def params(mebibytes=2):
    return pltpu.CompilerParams(vmem_limit_bytes=mebibytes * 2**20)


def in_hbm(a):
    return pltpu.with_memory_space_constraint(a, pltpu.HBM)


def turn(values, shift, axis):
    size = values.shape[axis]
    shift = shift % size
    return values if shift == 0 else pltpu.roll(values, shift, axis)


def primitives(rho, mx, my, mz, energy):
    inverse = 1.0 / rho
    u, v, w = mx * inverse, my * inverse, mz * inverse
    pressure = gamma_less * (energy - 0.5 * (mx * u + my * v + mz * w))
    return u, v, w, pressure


def east_fields(mx, my, mz, energy, u, v, w, p):
    return mx, mx * u + p, my * u, mz * u, (energy + p) * u, v, w


def north_fields(mx, my, mz, energy, u, v, w, p):
    return my, mx * v, my * v + p, mz * v, (energy + p) * v, u, w


def up_fields(mz, energy, u, v, w, p):
    return mz, mz * u, mz * v, mz * w + p, (energy + p) * w


def first_pack_kernel(state, low, high, y_low, y_high):
    for z in range(8):
        inverse = 1.0 / state[0, z]
        into = low if z < 4 else high
        into[0, z % 4] = state[1, z] * inverse
        into[1, z % 4] = state[2, z] * inverse
    sub = lax.broadcasted_iota(jnp.int32, (8, 128), 0)
    for c in range(5):
        for k in range(4):
            first, second = state[c, 2 * k, 0:8, :], state[c, 2 * k + 1, 0:8, :]
            y_low[c, k] = jnp.where(sub < 4, first, turn(second, 4, 0))
            first, second = state[c, 2 * k, 56:64, :], state[c, 2 * k + 1, 56:64, :]
            y_high[c, k] = jnp.where(sub < 4, turn(first, 4, 0), second)


def second_pack_kernel(state, x_low, x_high):
    lane = lax.broadcasted_iota(jnp.int32, (16, 128), 1)
    slot = lane >> 2
    for c in range(5):
        low = jnp.zeros((16, 128), f32)
        high = jnp.zeros((16, 128), f32)
        for j in range(32):
            row = j % 4 * 16
            moved = turn(state[c, j // 4, row : row + 16, :], 4 * j, 1)
            low = jnp.where(slot == j, moved, low)
            high = jnp.where(slot == (j - 1) % 32, moved, high)
        x_low[c] = low
        x_high[c] = high


def third_pack_kernel(state, low_b, high_b):
    for n, c in enumerate((0, 3, 4)):
        low_b[n] = state[c, :4]
        high_b[n] = state[c, 4:]


def split(f):
    high = f.astype(jnp.bfloat16)
    low = (f - high.astype(f32)).astype(jnp.bfloat16)
    return high, low


def write_circulant(matrix):
    row = lax.broadcasted_iota(jnp.int32, (128, 128), 0)
    column = lax.broadcasted_iota(jnp.int32, (128, 128), 1)
    offset = (row - column) & 127
    wide = jnp.zeros((128, 128), f32)
    for k in range(4):
        wide = jnp.where(offset == k + 1, weights[k], wide)
        wide = jnp.where(offset == 127 - k, -weights[k], wide)
    high, low = split(wide)
    for half in (slice(0, 128), slice(128, 256)):
        matrix[half, 0:128] = high
        matrix[half, 128:256] = low


def inner_kernel(state, from_south, from_north, partly, curls, matrix, yf, xf, dx):
    write_circulant(matrix)
    for ref, base in ((from_south, 4), (from_north, 72)):
        for k in range(4):
            rho, mx, my, mz, energy = (ref[c, k] for c in range(5))
            fields = north_fields(mx, my, mz, energy, *primitives(rho, mx, my, mz, energy))
            for n in range(7):
                yf[n, 2 * k, base : base + 4, :] = fields[n][0:4]
                yf[n, 2 * k + 1, base : base + 4, :] = fields[n][4:8]

    def plane(z, _):
        for r in range(0, 64, 16):
            rows = slice(r, r + 16)
            rho, mx, my, mz, energy = (state[c, z, rows, :] for c in range(5))
            parts = primitives(rho, mx, my, mz, energy)
            north = north_fields(mx, my, mz, energy, *parts)
            east = east_fields(mx, my, mz, energy, *parts)
            for n in range(7):
                yf[n, z, 8 + r : 24 + r, :] = north[n]
                high, low = split(east[n])
                xf[n, rows, 0:128] = high
                xf[n, rows, 128:256] = low
        for n in range(7):
            both = jnp.dot(xf[n], matrix[...], preferred_element_type=f32)
            dx[n] = both[:, 0:128] + both[:, 128:256]
        for r in range(0, 64, 16):
            rows = slice(r, r + 16)

            def along_y(n):
                total = None
                for k in range(4):
                    upper = yf[n, z, 9 + r + k : 25 + r + k, :]
                    lower = yf[n, z, 7 + r - k : 23 + r - k, :]
                    addend = weights[k] * (upper - lower)
                    total = addend if k == 0 else total + addend
                return total

            for c in range(5):
                partly[c, z, rows, :] = state[c, z, rows, :] - step_size * (dx[c, rows, :] + along_y(c))
            curls[0, z, rows, :] = along_y(6)
            curls[1, z, rows, :] = dx[6, rows, :]
            curls[2, z, rows, :] = dx[5, rows, :] - along_y(5)
        return 0

    lax.fori_loop(0, 8, plane, 0)


def edge_corrections(left_gap, right_gap):
    lane = lax.broadcasted_iota(jnp.int32, (16, 128), 1)
    place = lane & 3
    odd_slot = (lane >> 2 & 1) == 1
    left = jnp.zeros((16, 128), f32)
    right = jnp.zeros((16, 128), f32)
    for i in range(4):
        left += jnp.where(place + i <= 3, weights[3 - i], 0.0) * turn(left_gap, -i, 1)
        right += jnp.where(place >= i, weights[3 - i], 0.0) * turn(right_gap, i, 1)
    right = turn(right, -8, 1)
    return jnp.where(odd_slot, left, right), jnp.where(odd_slot, right, left)


def edge_pairs(fields, x_low, x_high, from_left, from_right):
    refs = (x_low, x_high, from_left, from_right)
    return [
        edge_corrections(high - left, right - low)
        for low, high, left, right in zip(*[fields(lambda c, ref=ref: ref[c]) for ref in refs])
    ]


def edge_tile(corrections, chunk):
    lane = lax.broadcasted_iota(jnp.int32, (16, 128), 1)
    fix = turn(corrections[chunk % 2], -4 * (chunk - 1), 1)
    return jnp.where(jnp.logical_or(lane < 4, lane >= 124), fix, 0.0)


def render_kernel(
    ray_total,
    grp,
    index,
    flip,
    density_of,
    curls,
    x_low,
    x_high,
    left_in,
    right_in,
    below_a,
    above_a,
    tables,
    sent,
    spins,
    uv,
    looked,
    from_left,
    from_right,
    sems,
):
    copies = [
        pltpu.make_async_copy(below_a, uv.at[:, 0:4], sems.at[0]),
        pltpu.make_async_copy(above_a, uv.at[:, 12:16], sems.at[1]),
        pltpu.make_async_copy(left_in, from_left, sems.at[2]),
        pltpu.make_async_copy(right_in, from_right, sems.at[3]),
    ]
    for copy in copies:
        copy.start()
    edges_of = (x_low, x_high, from_left, from_right)
    def own_plane(z, _):
        for r in range(0, 64, 16):
            rows = slice(r, r + 16)
            inverse = 1.0 / density_of[0, z, rows, :]
            uv[0, z + 4, rows, :] = density_of[1, z, rows, :] * inverse
            uv[1, z + 4, rows, :] = density_of[2, z, rows, :] * inverse
        return 0

    lax.fori_loop(0, 8, own_plane, 0)

    def coarse(read, i, m):
        gathered = None
        for dz in range(2):
            for dy in range(2):
                part = read(2 * i + dz, pl.ds(2 * m + dy, 8, stride=8))
                gathered = part if gathered is None else gathered + part
        return (gathered + turn(gathered, -1, 1)) * 0.125

    for i in range(4):
        chosen = index[4 * grp[0] + i]
        halves = []
        for c in range(4):
            first = jnp.broadcast_to(tables[chosen, c : c + 1, 0:128], (8, 128))
            second = jnp.broadcast_to(tables[chosen, c : c + 1, 128:256], (8, 128))
            last = lax.broadcasted_iota(jnp.int32, (8, 128), 1) == 127
            after_first = jnp.where(last, turn(second, -1, 1), turn(first, -1, 1))
            after_second = jnp.where(last, second, turn(second, -1, 1))
            halves.append((first, second, after_first - first, after_second - second))
        for m in range(4):
            density = coarse(lambda z, rows: density_of[0, z, rows, :], i, m)
            coord = 255.0 * jnp.clip((density - 0.9) / 0.6, 0.0, 1.0)
            cell = jnp.minimum(coord.astype(jnp.int32), 255)
            part = coord - cell.astype(f32)
            low_half = cell < 128
            entry = cell & 127

            def look(a, b):
                return jnp.where(
                    low_half,
                    jnp.take_along_axis(a, entry, axis=1),
                    jnp.take_along_axis(b, entry, axis=1),
                )

            for c, h in enumerate(halves):
                looked[i, m, c] = look(h[0], h[1]) + part * look(h[2], h[3])

    for copy in copies[2:]:
        copy.wait()

    def crossing(read):
        inverse = 1.0 / read(0)
        return read(2) * inverse, read(3) * inverse

    v_edge, w_edge = edge_pairs(crossing, *edges_of)
    for copy in copies[:2]:
        copy.wait()

    def depth(c, z, rows):
        total = None
        for k in range(4):
            addend = weights[k] * (uv[c, z + 5 + k, rows, :] - uv[c, z + 3 - k, rows, :])
            total = addend if k == 0 else total + addend
        return total

    for z in range(8):
        for b in range(4):
            rows = slice(16 * b, 16 * b + 16)
            chunk = 4 * z + b
            first = curls[0, z, rows, :] - depth(1, z, rows)
            second = depth(0, z, rows) - (curls[1, z, rows, :] + edge_tile(w_edge, chunk))
            third = curls[2, z, rows, :] + edge_tile(v_edge, chunk)
            spins[z, rows, :] = jnp.sqrt(first * first + second * second + third * third)

    lanes = lax.broadcasted_iota(jnp.int32, (8, 128), 1)
    rows_of = lax.broadcasted_iota(jnp.int32, (8, 128), 0)
    piece_lane = 16 * rows_of + 2 * (lanes & 7)
    outgoing = jnp.zeros((8, 128), f32)
    flipped = spread_flip(flip, lanes >> 1) == 1
    for i in range(4):
        total = None
        for m in range(4):
            spin = coarse(lambda z, rows: spins[z, rows, :], i, m)
            entries = [looked[i, m, c] for c in range(4)]
            opacity = opacity_gain * entries[3] * spin / (1.0 + spin) / ray_total
            piece = [entries[c] * opacity for c in range(3)] + [1.0 - opacity]
            total = piece if total is None else joined(total, piece, flipped)
        for span in (1, 2, 4):
            later = [turn(t, -span, 0) for t in total]
            total = joined(total, later, flipped)
        for c in range(4):
            row = jnp.broadcast_to(total[c][0:1, :], (8, 128))
            row = jnp.take_along_axis(row, piece_lane, axis=1)
            outgoing = jnp.where(lanes >> 3 == 4 * i + c, row, outgoing)
    sent[...] = outgoing


def spread_flip(flip, lane):
    both = jnp.concatenate([flip[...], flip[...]], axis=1)
    return jnp.take_along_axis(jnp.broadcast_to(both, lane.shape), lane, axis=1)


def joined(near, far, flipped):
    colors = [
        jnp.where(flipped, far[c] + far[3] * near[c], near[c] + near[3] * far[c]) for c in range(3)
    ]
    return colors + [near[3] * far[3]]


def depth_kernel(partly, state, *refs):
    edges_of, out, fz = refs[:4], refs[4], refs[5]
    for z in range(8):
        for r in range(0, 64, 16):
            rows = slice(r, r + 16)
            rho, mx, my, mz, energy = (state[c, z, rows, :] for c in range(5))
            fields = up_fields(mz, energy, *primitives(rho, mx, my, mz, energy))
            for c in range(5):
                fz[c, z, rows, :] = fields[c]

    def packed(read):
        rho, mx, my, mz, energy = (read(c) for c in range(5))
        return east_fields(mx, my, mz, energy, *primitives(rho, mx, my, mz, energy))[:5]

    edges = edge_pairs(packed, *edges_of)
    for c in range(5):
        for z in range(8):
            for b in range(4):
                rows = slice(16 * b, 16 * b + 16)
                total = edge_tile(edges[c], 4 * z + b)
                for k in range(4):
                    if z + k + 1 < 8:
                        total = total + weights[k] * fz[c, z + k + 1, rows, :]
                    if z - k - 1 >= 0:
                        total = total - weights[k] * fz[c, z - k - 1, rows, :]
                out[c, z, rows, :] = partly[c, z, rows, :] - step_size * total


def last_kernel(partly, *refs):
    below_in, below_b, above_in, above_b, out, fz, held, below_a, above_a, sems, out_sems = refs
    copies = [
        pltpu.make_async_copy(below_in, below_a, sems.at[0]),
        pltpu.make_async_copy(above_in, above_a, sems.at[1]),
    ]
    for copy in copies:
        copy.start()
    for copy in copies:
        copy.wait()

    def sending(c):
        return pltpu.make_async_copy(held.at[c], out.at[c], out_sems.at[c])

    for side, (a, b) in enumerate(((below_a, below_b), (above_a, above_b))):
        for p in range(4):
            for r in range(0, 64, 16):
                rows = slice(r, r + 16)
                u, v = a[0, p, rows, :], a[1, p, rows, :]
                rho, mz, energy = b[0, p, rows, :], b[1, p, rows, :], b[2, p, rows, :]
                w = mz / rho
                pressure = gamma_less * (energy - 0.5 * (rho * (u * u + v * v) + mz * w))
                fields = up_fields(mz, energy, u, v, w, pressure)
                for c in range(5):
                    fz[c, 4 * side + p, rows, :] = step_size * fields[c]
    for c in range(5):
        for z in range(8):
            for r in range(0, 64, 16):
                rows = slice(r, r + 16)
                total = partly[c, z, rows, :]
                for k in range(4):
                    if z + k + 1 >= 8:
                        total = total - weights[k] * fz[c, 4 + z + k + 1 - 8, rows, :]
                    if z - k - 1 < 0:
                        total = total + weights[k] * fz[c, z - k - 1 + 4, rows, :]
                held[c, z, rows, :] = total
        sending(c).start()
    for c in range(5):
        sending(c).wait()


def compose_kernel(depth, flip, pieces, out):
    lane = lax.broadcasted_iota(jnp.int32, (8, 128), 1)[0:1]
    channel = lane >> 3 & 3
    lanes = lax.broadcasted_iota(jnp.int32, (8, 128), 1)
    flipped = spread_flip(flip, 8 * depth[0] + (lanes & 7))[0:1] == 1

    def passing(x):
        second = jnp.where(channel == 1, turn(x, -16, 1), turn(x, -24, 1))
        return jnp.where(channel == 3, x, jnp.where(channel == 2, turn(x, -8, 1), second))

    total = pieces[0:1, :]
    total_pass = passing(total)
    for j in range(1, 8):
        later = pieces[j : j + 1, :]
        later_pass = passing(later)
        both = total_pass * later_pass
        color = jnp.where(flipped, later + later_pass * total, total + total_pass * later)
        total = jnp.where(channel == 3, both, color)
        total_pass = both
    out[...] = jnp.where(channel == 3, 1.0 - total, total)


def slot_kernel(me, owner, own, first, second, third, out, rows):
    for k, ref in enumerate((own, first, second, third)):
        rows[pl.ds((me[0] - k) & 3, 1), :] = ref[...]
    total = rows[...]
    sub = lax.broadcasted_iota(jnp.int32, (8, 128), 0)
    result = jnp.zeros((8, 128), f32)
    count = jnp.int32(0)
    shifted = [turn(total, -32 * i, 1) for i in range(4)]
    for b in range(16):
        mine = owner[b] == me[0]
        slot = jnp.where(mine, count, -1)
        count = jnp.where(mine, count + 1, count)
        row = jnp.broadcast_to(shifted[b % 4][b // 4 : b // 4 + 1, :], (8, 128))
        result = jnp.where(sub == slot, row, result)
    for c in range(4):
        out[:, c, :] = turn(result, -8 * c, 1)[:, 0:8]


def shape(*dims):
    return jax.ShapeDtypeStruct(dims, f32)


def ring(axis, step):
    count = lax.axis_size(axis)
    return [(i, (i + step) % count) for i in range(count)]


def after(value, *others):
    return lax.optimization_barrier((value, *others))[0]


def local(state, tf_table, owner, tf_index, view_flip):
    grp = lax.axis_index("grp")
    gy = lax.axis_index("gy")
    groups, depth = lax.axis_size("grp"), lax.axis_size("gy")
    low_a, high_a, y_low, y_high = pl.pallas_call(
        first_pack_kernel,
        out_shape=(shape(2, 4, 64, 128), shape(2, 4, 64, 128), shape(5, 4, 8, 128), shape(5, 4, 8, 128)),
        in_specs=[VM],
        out_specs=(VM, VM, VM, VM),
        compiler_params=params(),
    )(state)
    from_below_a = lax.ppermute(high_a, "grp", ring("grp", 1))
    from_above_a = lax.ppermute(low_a, "grp", ring("grp", -1))
    from_south = lax.ppermute(y_high, "gy", ring("gy", 1))
    from_north = lax.ppermute(y_low, "gy", ring("gy", -1))
    x_low, x_high = pl.pallas_call(
        second_pack_kernel,
        out_shape=(shape(5, 16, 128), shape(5, 16, 128)),
        in_specs=[VM],
        out_specs=(VM, VM),
        compiler_params=params(),
    )(after(state, y_low))
    from_left = lax.ppermute(x_high, "gx", ring("gx", 1))
    from_right = lax.ppermute(x_low, "gx", ring("gx", -1))
    partly, curls = pl.pallas_call(
        inner_kernel,
        out_shape=(shape(5, 8, 64, 128), shape(3, 8, 64, 128)),
        in_specs=[VM, VM, VM],
        out_specs=(VM, VM),
        scratch_shapes=[
            pltpu.VMEM((256, 256), jnp.bfloat16),
            pltpu.VMEM((7, 8, 80, 128), f32),
            pltpu.VMEM((7, 64, 256), jnp.bfloat16),
            pltpu.VMEM((7, 64, 128), f32),
        ],
        compiler_params=params(12),
        cost_estimate=weight(0.3),
    )(state, from_south, from_north)

    low_b, high_b = pl.pallas_call(
        third_pack_kernel,
        out_shape=(shape(3, 4, 64, 128), shape(3, 4, 64, 128)),
        in_specs=[VM],
        out_specs=(VM, VM),
        compiler_params=params(),
        cost_estimate=weight(0.3),
    )(after(state, x_low))
    low_b, high_b = lax.optimization_barrier((low_b, high_b, from_above_a, from_below_a))[:2]
    from_above_b = lax.ppermute(low_b, "grp", ring("grp", -1))
    from_below_b = lax.ppermute(high_b, "grp", ring("grp", 1))

    flip = view_flip[None, :]
    sent = pl.pallas_call(
        functools.partial(render_kernel, float(depth * 32)),
        out_shape=shape(8, 128),
        in_specs=[SM] * 2 + [VM] * 5 + [HB] * 4 + [VM],
        out_specs=VM,
        scratch_shapes=[
            pltpu.VMEM((8, 64, 128), f32),
            pltpu.VMEM((2, 16, 64, 128), f32),
            pltpu.VMEM((4, 4, 4, 8, 128), f32),
            pltpu.VMEM((5, 16, 128), f32),
            pltpu.VMEM((5, 16, 128), f32),
            pltpu.SemaphoreType.DMA((4,)),
        ],
        compiler_params=params(4),
        cost_estimate=weight(60),
    )(
        grp[None], tf_index, flip, state, curls,
        x_low, x_high, from_left, from_right, in_hbm(from_below_a), in_hbm(from_above_a), tf_table,
    )
    received = lax.all_to_all(sent, "gy", 0, 0, tiled=True)
    most = pl.pallas_call(
        depth_kernel,
        out_shape=shape(5, 8, 64, 128),
        in_specs=[VM] * 6,
        out_specs=VM,
        scratch_shapes=[pltpu.VMEM((5, 8, 64, 128), f32)],
        compiler_params=params(6),
    )(after(partly, sent), state, x_low, x_high, from_left, from_right)
    rays = pl.pallas_call(
        compose_kernel,
        out_shape=shape(1, 128),
        in_specs=[SM, VM, VM],
        out_specs=VM,
        compiler_params=params(),
    )(gy[None], flip, after(received, most))
    others = [lax.ppermute(rays, "grp", ring("grp", k)) for k in range(1, groups)]
    new_state = pl.pallas_call(
        last_kernel,
        out_shape=shape(5, 8, 64, 128),
        in_specs=[VM, HB, VM, HB, VM],
        out_specs=HB,
        scratch_shapes=[
            pltpu.VMEM((5, 8, 64, 128), f32),
            pltpu.VMEM((5, 8, 64, 128), f32),
            pltpu.VMEM((2, 4, 64, 128), f32),
            pltpu.VMEM((2, 4, 64, 128), f32),
            pltpu.SemaphoreType.DMA((2,)),
            pltpu.SemaphoreType.DMA((5,)),
        ],
        compiler_params=params(6),
    )(most, in_hbm(from_below_a), from_below_b, in_hbm(from_above_a), from_above_b)
    image = pl.pallas_call(
        slot_kernel,
        out_shape=shape(8, 4, 8),
        in_specs=[SM, SM] + [VM] * 4,
        out_specs=VM,
        scratch_shapes=[pltpu.VMEM((4, 128), f32)],
        compiler_params=params(),
    )(grp[None], owner[:, 0], after(rays, new_state), *others)
    return (new_state, image)


def solution(mesh):
    placed = (P(None, "grp", "gy", "gx"), P(), P(), P(), P("gx"))
    return jax.shard_map(
        local,
        mesh=mesh,
        in_specs=placed,
        out_specs=(P(None, "grp", "gy", "gx"), P("grp", None, ("gx", "gy"))),
        check_vma=False,
    )
```

```python
import functools

import jax
import jax.numpy as jnp
from jax import lax
from jax.experimental import pallas as pl
from jax.experimental.pallas import tpu as pltpu
from jax.sharding import PartitionSpec as P

gamma_less = 0.4
step_size = 0.5
opacity_gain = 6.0
w1, w2, w3, w4 = (0.8, -0.2, 4.0 / 105.0, -1.0 / 280.0)
weights = (w1, w2, w3, w4)

f32 = jnp.float32
VM = pl.BlockSpec(memory_space=pltpu.VMEM)
SM = pl.BlockSpec(memory_space=pltpu.SMEM)
HB = pl.BlockSpec(memory_space=pltpu.HBM)


def weight(microseconds):
    return pl.CostEstimate(flops=int(microseconds * 1e9), bytes_accessed=1000000, transcendentals=0)


def params(mebibytes=2):
    return pltpu.CompilerParams(vmem_limit_bytes=mebibytes * 2**20)


def in_hbm(a):
    return pltpu.with_memory_space_constraint(a, pltpu.HBM)


def turn(values, shift, axis):
    size = values.shape[axis]
    shift = shift % size
    return values if shift == 0 else pltpu.roll(values, shift, axis)


def primitives(rho, mx, my, mz, energy):
    inverse = 1.0 / rho
    u, v, w = mx * inverse, my * inverse, mz * inverse
    pressure = gamma_less * (energy - 0.5 * (mx * u + my * v + mz * w))
    return u, v, w, pressure


def east_fields(mx, my, mz, energy, u, v, w, p):
    return mx, mx * u + p, my * u, mz * u, (energy + p) * u, v, w


def north_fields(mx, my, mz, energy, u, v, w, p):
    return my, mx * v, my * v + p, mz * v, (energy + p) * v, u, w


def up_fields(mz, energy, u, v, w, p):
    return mz, mz * u, mz * v, mz * w + p, (energy + p) * w


def first_pack_kernel(state, low, high, held, sems):
    copies = [
        pltpu.make_async_copy(state.at[c, pl.ds(4 * h, 4)], held.at[c, pl.ds(4 * h, 4)], sems.at[3 * h + c])
        for h in range(2)
        for c in range(3)
    ]
    for copy in copies:
        copy.start()
    for h, into in enumerate((low, high)):
        for copy in copies[3 * h : 3 * h + 3]:
            copy.wait()
        for z in range(4):
            inverse = 1.0 / held[0, 4 * h + z]
            into[0, z] = held[1, 4 * h + z] * inverse
            into[1, z] = held[2, 4 * h + z] * inverse


def row_pack_kernel(state, y_low, y_high):
    sub = lax.broadcasted_iota(jnp.int32, (8, 128), 0)
    for c in range(5):
        for k in range(4):
            first, second = state[c, 2 * k, 0:8, :], state[c, 2 * k + 1, 0:8, :]
            y_low[c, k] = jnp.where(sub < 4, first, turn(second, 4, 0))
            first, second = state[c, 2 * k, 56:64, :], state[c, 2 * k + 1, 56:64, :]
            y_high[c, k] = jnp.where(sub < 4, turn(first, 4, 0), second)


def second_pack_kernel(state, x_low, x_high):
    lane = lax.broadcasted_iota(jnp.int32, (16, 128), 1)
    slot = lane >> 2
    for c in range(5):
        low = jnp.zeros((16, 128), f32)
        high = jnp.zeros((16, 128), f32)
        for j in range(32):
            row = j % 4 * 16
            moved = turn(state[c, j // 4, row : row + 16, :], 4 * j, 1)
            low = jnp.where(slot == j, moved, low)
            high = jnp.where(slot == (j - 1) % 32, moved, high)
        x_low[c] = low
        x_high[c] = high


def third_pack_kernel(state, low_b, high_b):
    for n, c in enumerate((0, 3, 4)):
        low_b[n] = state[c, :4]
        high_b[n] = state[c, 4:]


def split(f):
    high = f.astype(jnp.bfloat16)
    low = (f - high.astype(f32)).astype(jnp.bfloat16)
    return high, low


def write_circulant(matrix):
    row = lax.broadcasted_iota(jnp.int32, (128, 128), 0)
    column = lax.broadcasted_iota(jnp.int32, (128, 128), 1)
    offset = (row - column) & 127
    wide = jnp.zeros((128, 128), f32)
    for k in range(4):
        wide = jnp.where(offset == k + 1, weights[k], wide)
        wide = jnp.where(offset == 127 - k, -weights[k], wide)
    high, low = split(wide)
    for half in (slice(0, 128), slice(128, 256)):
        matrix[half, 0:128] = high
        matrix[half, 128:256] = low


def inner_kernel(state, from_south, from_north, partly, curls, matrix, yf, xf, dx):
    write_circulant(matrix)
    for ref, base in ((from_south, 4), (from_north, 72)):
        for k in range(4):
            rho, mx, my, mz, energy = (ref[c, k] for c in range(5))
            fields = north_fields(mx, my, mz, energy, *primitives(rho, mx, my, mz, energy))
            for n in range(7):
                yf[n, 2 * k, base : base + 4, :] = fields[n][0:4]
                yf[n, 2 * k + 1, base : base + 4, :] = fields[n][4:8]

    def plane(z, _):
        for r in range(0, 64, 16):
            rows = slice(r, r + 16)
            rho, mx, my, mz, energy = (state[c, z, rows, :] for c in range(5))
            parts = primitives(rho, mx, my, mz, energy)
            north = north_fields(mx, my, mz, energy, *parts)
            east = east_fields(mx, my, mz, energy, *parts)
            for n in range(7):
                yf[n, z, 8 + r : 24 + r, :] = north[n]
                high, low = split(east[n])
                xf[n, rows, 0:128] = high
                xf[n, rows, 128:256] = low
        for n in range(7):
            both = jnp.dot(xf[n], matrix[...], preferred_element_type=f32)
            dx[n] = both[:, 0:128] + both[:, 128:256]
        for r in range(0, 64, 16):
            rows = slice(r, r + 16)

            def along_y(n):
                total = None
                for k in range(4):
                    upper = yf[n, z, 9 + r + k : 25 + r + k, :]
                    lower = yf[n, z, 7 + r - k : 23 + r - k, :]
                    addend = weights[k] * (upper - lower)
                    total = addend if k == 0 else total + addend
                return total

            for c in range(5):
                partly[c, z, rows, :] = state[c, z, rows, :] - step_size * (dx[c, rows, :] + along_y(c))
            curls[0, z, rows, :] = along_y(6)
            curls[1, z, rows, :] = dx[6, rows, :]
            curls[2, z, rows, :] = dx[5, rows, :] - along_y(5)
        return 0

    lax.fori_loop(0, 8, plane, 0)


def edge_corrections(left_gap, right_gap):
    lane = lax.broadcasted_iota(jnp.int32, (16, 128), 1)
    place = lane & 3
    odd_slot = (lane >> 2 & 1) == 1
    left = jnp.zeros((16, 128), f32)
    right = jnp.zeros((16, 128), f32)
    for i in range(4):
        left += jnp.where(place + i <= 3, weights[3 - i], 0.0) * turn(left_gap, -i, 1)
        right += jnp.where(place >= i, weights[3 - i], 0.0) * turn(right_gap, i, 1)
    right = turn(right, -8, 1)
    return jnp.where(odd_slot, left, right), jnp.where(odd_slot, right, left)


def edge_pairs(fields, x_low, x_high, from_left, from_right):
    refs = (x_low, x_high, from_left, from_right)
    return [
        edge_corrections(high - left, right - low)
        for low, high, left, right in zip(*[fields(lambda c, ref=ref: ref[c]) for ref in refs])
    ]


def edge_tile(corrections, chunk):
    lane = lax.broadcasted_iota(jnp.int32, (16, 128), 1)
    fix = turn(corrections[chunk % 2], -4 * (chunk - 1), 1)
    return jnp.where(jnp.logical_or(lane < 4, lane >= 124), fix, 0.0)


def render_kernel(
    ray_total,
    grp,
    index,
    flip,
    density_of,
    curls,
    x_low,
    x_high,
    left_in,
    right_in,
    below_a,
    above_a,
    tables,
    sent,
    spins,
    uv,
    looked,
    from_left,
    from_right,
    sems,
):
    copies = [
        pltpu.make_async_copy(below_a, uv.at[:, 0:4], sems.at[0]),
        pltpu.make_async_copy(above_a, uv.at[:, 12:16], sems.at[1]),
        pltpu.make_async_copy(left_in, from_left, sems.at[2]),
        pltpu.make_async_copy(right_in, from_right, sems.at[3]),
    ]
    for copy in copies:
        copy.start()
    edges_of = (x_low, x_high, from_left, from_right)
    def own_plane(z, _):
        for r in range(0, 64, 16):
            rows = slice(r, r + 16)
            inverse = 1.0 / density_of[0, z, rows, :]
            uv[0, z + 4, rows, :] = density_of[1, z, rows, :] * inverse
            uv[1, z + 4, rows, :] = density_of[2, z, rows, :] * inverse
        return 0

    lax.fori_loop(0, 8, own_plane, 0)

    def coarse(read, i, m):
        gathered = None
        for dz in range(2):
            for dy in range(2):
                part = read(2 * i + dz, pl.ds(2 * m + dy, 8, stride=8))
                gathered = part if gathered is None else gathered + part
        return (gathered + turn(gathered, -1, 1)) * 0.125

    for i in range(4):
        chosen = index[4 * grp[0] + i]
        halves = []
        for c in range(4):
            first = jnp.broadcast_to(tables[chosen, c : c + 1, 0:128], (8, 128))
            second = jnp.broadcast_to(tables[chosen, c : c + 1, 128:256], (8, 128))
            last = lax.broadcasted_iota(jnp.int32, (8, 128), 1) == 127
            after_first = jnp.where(last, turn(second, -1, 1), turn(first, -1, 1))
            after_second = jnp.where(last, second, turn(second, -1, 1))
            halves.append((first, second, after_first - first, after_second - second))
        for m in range(4):
            density = coarse(lambda z, rows: density_of[0, z, rows, :], i, m)
            coord = 255.0 * jnp.clip((density - 0.9) / 0.6, 0.0, 1.0)
            cell = jnp.minimum(coord.astype(jnp.int32), 255)
            part = coord - cell.astype(f32)
            low_half = cell < 128
            entry = cell & 127

            def look(a, b):
                return jnp.where(
                    low_half,
                    jnp.take_along_axis(a, entry, axis=1),
                    jnp.take_along_axis(b, entry, axis=1),
                )

            for c, h in enumerate(halves):
                looked[i, m, c] = look(h[0], h[1]) + part * look(h[2], h[3])

    for copy in copies[2:]:
        copy.wait()

    def crossing(read):
        inverse = 1.0 / read(0)
        return read(2) * inverse, read(3) * inverse

    v_edge, w_edge = edge_pairs(crossing, *edges_of)
    for copy in copies[:2]:
        copy.wait()

    def depth(c, z, rows):
        total = None
        for k in range(4):
            addend = weights[k] * (uv[c, z + 5 + k, rows, :] - uv[c, z + 3 - k, rows, :])
            total = addend if k == 0 else total + addend
        return total

    for z in range(8):
        for b in range(4):
            rows = slice(16 * b, 16 * b + 16)
            chunk = 4 * z + b
            first = curls[0, z, rows, :] - depth(1, z, rows)
            second = depth(0, z, rows) - (curls[1, z, rows, :] + edge_tile(w_edge, chunk))
            third = curls[2, z, rows, :] + edge_tile(v_edge, chunk)
            spins[z, rows, :] = jnp.sqrt(first * first + second * second + third * third)

    lanes = lax.broadcasted_iota(jnp.int32, (8, 128), 1)
    rows_of = lax.broadcasted_iota(jnp.int32, (8, 128), 0)
    piece_lane = 16 * rows_of + 2 * (lanes & 7)
    outgoing = jnp.zeros((8, 128), f32)
    flipped = spread_flip(flip, lanes >> 1) == 1
    for i in range(4):
        total = None
        for m in range(4):
            spin = coarse(lambda z, rows: spins[z, rows, :], i, m)
            entries = [looked[i, m, c] for c in range(4)]
            opacity = opacity_gain * entries[3] * spin / (1.0 + spin) / ray_total
            piece = [entries[c] * opacity for c in range(3)] + [1.0 - opacity]
            total = piece if total is None else joined(total, piece, flipped)
        for span in (1, 2, 4):
            later = [turn(t, -span, 0) for t in total]
            total = joined(total, later, flipped)
        for c in range(4):
            row = jnp.broadcast_to(total[c][0:1, :], (8, 128))
            row = jnp.take_along_axis(row, piece_lane, axis=1)
            outgoing = jnp.where(lanes >> 3 == 4 * i + c, row, outgoing)
    for g in range(4):
        sent[8 * g : 8 * g + 8, :] = outgoing


def spread_flip(flip, lane):
    both = jnp.concatenate([flip[...], flip[...]], axis=1)
    return jnp.take_along_axis(jnp.broadcast_to(both, lane.shape), lane, axis=1)


def joined(near, far, flipped):
    colors = [
        jnp.where(flipped, far[c] + far[3] * near[c], near[c] + near[3] * far[c]) for c in range(3)
    ]
    return colors + [near[3] * far[3]]


def depth_kernel(partly, state, *refs):
    edges_of, out, fz = refs[:4], refs[4], refs[5]
    for z in range(8):
        for r in range(0, 64, 16):
            rows = slice(r, r + 16)
            rho, mx, my, mz, energy = (state[c, z, rows, :] for c in range(5))
            fields = up_fields(mz, energy, *primitives(rho, mx, my, mz, energy))
            for c in range(5):
                fz[c, z, rows, :] = fields[c]

    def packed(read):
        rho, mx, my, mz, energy = (read(c) for c in range(5))
        return east_fields(mx, my, mz, energy, *primitives(rho, mx, my, mz, energy))[:5]

    edges = edge_pairs(packed, *edges_of)
    for c in range(5):
        for z in range(8):
            for b in range(4):
                rows = slice(16 * b, 16 * b + 16)
                total = edge_tile(edges[c], 4 * z + b)
                for k in range(4):
                    if z + k + 1 < 8:
                        total = total + weights[k] * fz[c, z + k + 1, rows, :]
                    if z - k - 1 >= 0:
                        total = total - weights[k] * fz[c, z - k - 1, rows, :]
                out[c, z, rows, :] = partly[c, z, rows, :] - step_size * total


def last_kernel(partly, *refs):
    below_in, below_b, above_in, above_b, out, fz, held, below_a, above_a, sems, out_sems = refs
    copies = [
        pltpu.make_async_copy(below_in, below_a, sems.at[0]),
        pltpu.make_async_copy(above_in, above_a, sems.at[1]),
    ]
    for copy in copies:
        copy.start()
    for copy in copies:
        copy.wait()

    def sending(c):
        return pltpu.make_async_copy(held.at[c], out.at[c], out_sems.at[c])

    for side, (a, b) in enumerate(((below_a, below_b), (above_a, above_b))):
        for p in range(4):
            for r in range(0, 64, 16):
                rows = slice(r, r + 16)
                u, v = a[0, p, rows, :], a[1, p, rows, :]
                rho, mz, energy = b[0, p, rows, :], b[1, p, rows, :], b[2, p, rows, :]
                w = mz / rho
                pressure = gamma_less * (energy - 0.5 * (rho * (u * u + v * v) + mz * w))
                fields = up_fields(mz, energy, u, v, w, pressure)
                for c in range(5):
                    fz[c, 4 * side + p, rows, :] = step_size * fields[c]
    for c in range(5):
        for z in range(8):
            for r in range(0, 64, 16):
                rows = slice(r, r + 16)
                total = partly[c, z, rows, :]
                for k in range(4):
                    if z + k + 1 >= 8:
                        total = total - weights[k] * fz[c, 4 + z + k + 1 - 8, rows, :]
                    if z - k - 1 < 0:
                        total = total + weights[k] * fz[c, z - k - 1 + 4, rows, :]
                held[c, z, rows, :] = total
        sending(c).start()
    for c in range(5):
        sending(c).wait()


def compose_kernel(me, depth, owner, flip, pieces, out):
    lane = lax.broadcasted_iota(jnp.int32, (4, 128), 1)
    channel = lane >> 3 & 3
    lanes = lax.broadcasted_iota(jnp.int32, (8, 128), 1)
    flipped = spread_flip(flip, 8 * depth[0] + (lanes & 7))[0:4] == 1

    def passing(x):
        return jnp.where(
            channel == 3,
            x,
            jnp.where(
                channel == 2, turn(x, -8, 1), jnp.where(channel == 1, turn(x, -16, 1), turn(x, -24, 1))
            ),
        )

    total = pieces[:, 0, :]
    total_pass = passing(total)
    for j in range(1, 8):
        later = pieces[:, j, :]
        later_pass = passing(later)
        both = total_pass * later_pass
        color = jnp.where(flipped, later + later_pass * total, total + total_pass * later)
        total = jnp.where(channel == 3, both, color)
        total_pass = both
    total = jnp.where(channel == 3, 1.0 - total, total)
    sub = lax.broadcasted_iota(jnp.int32, (8, 128), 0)
    result = jnp.zeros((8, 128), f32)
    count = jnp.int32(0)
    shifted = [turn(total, -32 * i, 1) for i in range(4)]
    for b in range(16):
        mine = owner[b] == me[0]
        slot = jnp.where(mine, count, -1)
        count = jnp.where(mine, count + 1, count)
        row = jnp.broadcast_to(shifted[b % 4][b // 4 : b // 4 + 1, :], (8, 128))
        result = jnp.where(sub == slot, row, result)
    for c in range(4):
        out[:, c, :] = turn(result, -8 * c, 1)[:, 0:8]


def shape(*dims):
    return jax.ShapeDtypeStruct(dims, f32)


def ring(axis, step):
    count = lax.axis_size(axis)
    return [(i, (i + step) % count) for i in range(count)]


def after(value, *others):
    return lax.optimization_barrier((value, *others))[0]


def local(state, tf_table, owner, tf_index, view_flip):
    grp = lax.axis_index("grp")
    gy = lax.axis_index("gy")
    groups, depth = lax.axis_size("grp"), lax.axis_size("gy")
    low_a, high_a = pl.pallas_call(
        first_pack_kernel,
        out_shape=(shape(2, 4, 64, 128), shape(2, 4, 64, 128)),
        in_specs=[HB],
        out_specs=(VM, VM),
        scratch_shapes=[pltpu.VMEM((3, 8, 64, 128), f32), pltpu.SemaphoreType.DMA((6,))],
        compiler_params=params(),
    )(in_hbm(state))
    y_low, y_high = pl.pallas_call(
        row_pack_kernel,
        out_shape=(shape(5, 4, 8, 128), shape(5, 4, 8, 128)),
        in_specs=[VM],
        out_specs=(VM, VM),
        compiler_params=params(),
    )(after(state, low_a))
    from_below_a = lax.ppermute(high_a, "grp", ring("grp", 1))
    from_above_a = lax.ppermute(low_a, "grp", ring("grp", -1))
    from_south = lax.ppermute(y_high, "gy", ring("gy", 1))
    from_north = lax.ppermute(y_low, "gy", ring("gy", -1))
    x_low, x_high = pl.pallas_call(
        second_pack_kernel,
        out_shape=(shape(5, 16, 128), shape(5, 16, 128)),
        in_specs=[VM],
        out_specs=(VM, VM),
        compiler_params=params(),
    )(after(state, y_low))
    from_left = lax.ppermute(x_high, "gx", ring("gx", 1))
    from_right = lax.ppermute(x_low, "gx", ring("gx", -1))
    partly, curls = pl.pallas_call(
        inner_kernel,
        out_shape=(shape(5, 8, 64, 128), shape(3, 8, 64, 128)),
        in_specs=[VM, VM, VM],
        out_specs=(VM, VM),
        scratch_shapes=[
            pltpu.VMEM((256, 256), jnp.bfloat16),
            pltpu.VMEM((7, 8, 80, 128), f32),
            pltpu.VMEM((7, 64, 256), jnp.bfloat16),
            pltpu.VMEM((7, 64, 128), f32),
        ],
        compiler_params=params(12),
        cost_estimate=weight(0.3),
    )(state, from_south, from_north)

    low_b, high_b = pl.pallas_call(
        third_pack_kernel,
        out_shape=(shape(3, 4, 64, 128), shape(3, 4, 64, 128)),
        in_specs=[VM],
        out_specs=(VM, VM),
        compiler_params=params(),
        cost_estimate=weight(0.3),
    )(after(state, x_low))
    low_b, high_b = lax.optimization_barrier((low_b, high_b, from_above_a, from_below_a))[:2]
    from_above_b = lax.ppermute(low_b, "grp", ring("grp", -1))
    from_below_b = lax.ppermute(high_b, "grp", ring("grp", 1))

    flip = view_flip[None, :]
    sent = pl.pallas_call(
        functools.partial(render_kernel, float(depth * 32)),
        out_shape=shape(32, 128),
        in_specs=[SM] * 2 + [VM] * 5 + [HB] * 4 + [VM],
        out_specs=VM,
        scratch_shapes=[
            pltpu.VMEM((8, 64, 128), f32),
            pltpu.VMEM((2, 16, 64, 128), f32),
            pltpu.VMEM((4, 4, 4, 8, 128), f32),
            pltpu.VMEM((5, 16, 128), f32),
            pltpu.VMEM((5, 16, 128), f32),
            pltpu.SemaphoreType.DMA((4,)),
        ],
        compiler_params=params(4),
        cost_estimate=weight(60),
    )(
        grp[None], tf_index, flip, state, curls,
        x_low, x_high, from_left, from_right, in_hbm(from_below_a), in_hbm(from_above_a), tf_table,
    )
    received = lax.all_to_all(sent, ("grp", "gy"), 0, 0, tiled=True).reshape(groups, depth, 128)
    most = pl.pallas_call(
        depth_kernel,
        out_shape=shape(5, 8, 64, 128),
        in_specs=[VM] * 6,
        out_specs=VM,
        scratch_shapes=[pltpu.VMEM((5, 8, 64, 128), f32)],
        compiler_params=params(6),
    )(after(partly, sent), state, x_low, x_high, from_left, from_right)
    new_state = pl.pallas_call(
        last_kernel,
        out_shape=shape(5, 8, 64, 128),
        in_specs=[VM, HB, VM, HB, VM],
        out_specs=HB,
        scratch_shapes=[
            pltpu.VMEM((5, 8, 64, 128), f32),
            pltpu.VMEM((5, 8, 64, 128), f32),
            pltpu.VMEM((2, 4, 64, 128), f32),
            pltpu.VMEM((2, 4, 64, 128), f32),
            pltpu.SemaphoreType.DMA((2,)),
            pltpu.SemaphoreType.DMA((5,)),
        ],
        compiler_params=params(6),
    )(most, in_hbm(from_below_a), from_below_b, in_hbm(from_above_a), from_above_b)
    image = pl.pallas_call(
        compose_kernel,
        out_shape=shape(8, 4, 8),
        in_specs=[SM, SM, SM, VM, VM],
        out_specs=VM,
        compiler_params=params(),
    )(grp[None], gy[None], owner[:, 0], flip, after(received, new_state))
    return (new_state, image)


def solution(mesh):
    placed = (P(None, "grp", "gy", "gx"), P(), P(), P(), P("gx"))
    return jax.shard_map(
        local,
        mesh=mesh,
        in_specs=placed,
        out_specs=(P(None, "grp", "gy", "gx"), P("grp", None, ("gx", "gy"))),
        check_vma=False,
    )
```

```python
import functools

import jax
import jax.numpy as jnp
from jax import lax
from jax.experimental import pallas as pl
from jax.experimental.pallas import tpu as pltpu
from jax.sharding import PartitionSpec as P

gamma_less = 0.4
step_size = 0.5
opacity_gain = 6.0
w1, w2, w3, w4 = (0.8, -0.2, 4.0 / 105.0, -1.0 / 280.0)
weights = (w1, w2, w3, w4)

f32 = jnp.float32
VM = pl.BlockSpec(memory_space=pltpu.VMEM)
SM = pl.BlockSpec(memory_space=pltpu.SMEM)
HB = pl.BlockSpec(memory_space=pltpu.HBM)


def weight(microseconds):
    return pl.CostEstimate(flops=int(microseconds * 1e9), bytes_accessed=1000000, transcendentals=0)


def params(mebibytes=2):
    return pltpu.CompilerParams(vmem_limit_bytes=mebibytes * 2**20)


def in_hbm(a):
    return pltpu.with_memory_space_constraint(a, pltpu.HBM)


def turn(values, shift, axis):
    size = values.shape[axis]
    shift = shift % size
    return values if shift == 0 else pltpu.roll(values, shift, axis)


def primitives(rho, mx, my, mz, energy):
    inverse = 1.0 / rho
    u, v, w = mx * inverse, my * inverse, mz * inverse
    pressure = gamma_less * (energy - 0.5 * (mx * u + my * v + mz * w))
    return u, v, w, pressure


def east_fields(mx, my, mz, energy, u, v, w, p):
    return mx, mx * u + p, my * u, mz * u, (energy + p) * u, v, w


def north_fields(mx, my, mz, energy, u, v, w, p):
    return my, mx * v, my * v + p, mz * v, (energy + p) * v, u, w


def up_fields(mz, energy, u, v, w, p):
    return mz, mz * u, mz * v, mz * w + p, (energy + p) * w


def first_pack_kernel(state, low, high, held, sems):
    copies = [
        pltpu.make_async_copy(state.at[c, pl.ds(4 * h, 4)], held.at[c, pl.ds(4 * h, 4)], sems.at[3 * h + c])
        for h in range(2)
        for c in range(3)
    ]
    for copy in copies:
        copy.start()
    for h, into in enumerate((low, high)):
        for copy in copies[3 * h : 3 * h + 3]:
            copy.wait()
        for z in range(4):
            inverse = 1.0 / held[0, 4 * h + z]
            into[0, z] = held[1, 4 * h + z] * inverse
            into[1, z] = held[2, 4 * h + z] * inverse


def row_pack_kernel(state, y_low, y_high):
    sub = lax.broadcasted_iota(jnp.int32, (8, 128), 0)
    for c in range(5):
        for k in range(4):
            first, second = state[c, 2 * k, 0:8, :], state[c, 2 * k + 1, 0:8, :]
            y_low[c, k] = jnp.where(sub < 4, first, turn(second, 4, 0))
            first, second = state[c, 2 * k, 56:64, :], state[c, 2 * k + 1, 56:64, :]
            y_high[c, k] = jnp.where(sub < 4, turn(first, 4, 0), second)


def second_pack_kernel(state, x_low, x_high):
    lane = lax.broadcasted_iota(jnp.int32, (16, 128), 1)
    slot = lane >> 2
    for c in range(5):
        low = jnp.zeros((16, 128), f32)
        high = jnp.zeros((16, 128), f32)
        for j in range(32):
            row = j % 4 * 16
            moved = turn(state[c, j // 4, row : row + 16, :], 4 * j, 1)
            low = jnp.where(slot == j, moved, low)
            high = jnp.where(slot == (j - 1) % 32, moved, high)
        x_low[c] = low
        x_high[c] = high


def third_pack_kernel(state, low_b, high_b):
    for n, c in enumerate((0, 3, 4)):
        low_b[n] = state[c, :4]
        high_b[n] = state[c, 4:]


def split(f):
    high = f.astype(jnp.bfloat16)
    low = (f - high.astype(f32)).astype(jnp.bfloat16)
    return high, low


def write_circulant(matrix):
    row = lax.broadcasted_iota(jnp.int32, (128, 128), 0)
    column = lax.broadcasted_iota(jnp.int32, (128, 128), 1)
    offset = (row - column) & 127
    wide = jnp.zeros((128, 128), f32)
    for k in range(4):
        wide = jnp.where(offset == k + 1, weights[k], wide)
        wide = jnp.where(offset == 127 - k, -weights[k], wide)
    high, low = split(wide)
    for half in (slice(0, 128), slice(128, 256)):
        matrix[half, 0:128] = high
        matrix[half, 128:256] = low


def inner_kernel(state, from_south, from_north, partly, curls, matrix, yf, xf, dx):
    write_circulant(matrix)
    for ref, base in ((from_south, 4), (from_north, 72)):
        for k in range(4):
            rho, mx, my, mz, energy = (ref[c, k] for c in range(5))
            fields = north_fields(mx, my, mz, energy, *primitives(rho, mx, my, mz, energy))
            for n in range(7):
                yf[n, 2 * k, base : base + 4, :] = fields[n][0:4]
                yf[n, 2 * k + 1, base : base + 4, :] = fields[n][4:8]

    def plane(z, _):
        for r in range(0, 64, 16):
            rows = slice(r, r + 16)
            rho, mx, my, mz, energy = (state[c, z, rows, :] for c in range(5))
            parts = primitives(rho, mx, my, mz, energy)
            north = north_fields(mx, my, mz, energy, *parts)
            east = east_fields(mx, my, mz, energy, *parts)
            for n in range(7):
                yf[n, z, 8 + r : 24 + r, :] = north[n]
                high, low = split(east[n])
                xf[n, rows, 0:128] = high
                xf[n, rows, 128:256] = low
        for n in range(7):
            both = jnp.dot(xf[n], matrix[...], preferred_element_type=f32)
            dx[n] = both[:, 0:128] + both[:, 128:256]
        for r in range(0, 64, 16):
            rows = slice(r, r + 16)

            def along_y(n):
                total = None
                for k in range(4):
                    upper = yf[n, z, 9 + r + k : 25 + r + k, :]
                    lower = yf[n, z, 7 + r - k : 23 + r - k, :]
                    addend = weights[k] * (upper - lower)
                    total = addend if k == 0 else total + addend
                return total

            for c in range(5):
                partly[c, z, rows, :] = state[c, z, rows, :] - step_size * (dx[c, rows, :] + along_y(c))
            curls[0, z, rows, :] = along_y(6)
            curls[1, z, rows, :] = dx[6, rows, :]
            curls[2, z, rows, :] = dx[5, rows, :] - along_y(5)
        return 0

    lax.fori_loop(0, 8, plane, 0)


def edge_corrections(left_gap, right_gap):
    lane = lax.broadcasted_iota(jnp.int32, (16, 128), 1)
    place = lane & 3
    odd_slot = (lane >> 2 & 1) == 1
    left = jnp.zeros((16, 128), f32)
    right = jnp.zeros((16, 128), f32)
    for i in range(4):
        left += jnp.where(place + i <= 3, weights[3 - i], 0.0) * turn(left_gap, -i, 1)
        right += jnp.where(place >= i, weights[3 - i], 0.0) * turn(right_gap, i, 1)
    right = turn(right, -8, 1)
    return jnp.where(odd_slot, left, right), jnp.where(odd_slot, right, left)


def edge_pairs(fields, x_low, x_high, from_left, from_right):
    refs = (x_low, x_high, from_left, from_right)
    return [
        edge_corrections(high - left, right - low)
        for low, high, left, right in zip(*[fields(lambda c, ref=ref: ref[c]) for ref in refs])
    ]


def edge_tile(corrections, chunk):
    lane = lax.broadcasted_iota(jnp.int32, (16, 128), 1)
    fix = turn(corrections[chunk % 2], -4 * (chunk - 1), 1)
    return jnp.where(jnp.logical_or(lane < 4, lane >= 124), fix, 0.0)


def render_kernel(
    ray_total,
    grp,
    index,
    flip,
    density_of,
    curls,
    x_low,
    x_high,
    left_in,
    right_in,
    below_a,
    above_a,
    tables,
    sent,
    spins,
    uv,
    looked,
    from_left,
    from_right,
    sems,
):
    copies = [
        pltpu.make_async_copy(below_a, uv.at[:, 0:4], sems.at[0]),
        pltpu.make_async_copy(above_a, uv.at[:, 12:16], sems.at[1]),
        pltpu.make_async_copy(left_in, from_left, sems.at[2]),
        pltpu.make_async_copy(right_in, from_right, sems.at[3]),
    ]
    for copy in copies:
        copy.start()
    edges_of = (x_low, x_high, from_left, from_right)
    def own_plane(z, _):
        for r in range(0, 64, 16):
            rows = slice(r, r + 16)
            inverse = 1.0 / density_of[0, z, rows, :]
            uv[0, z + 4, rows, :] = density_of[1, z, rows, :] * inverse
            uv[1, z + 4, rows, :] = density_of[2, z, rows, :] * inverse
        return 0

    lax.fori_loop(0, 8, own_plane, 0)

    def coarse(read, i, m):
        gathered = None
        for dz in range(2):
            for dy in range(2):
                part = read(2 * i + dz, pl.ds(2 * m + dy, 8, stride=8))
                gathered = part if gathered is None else gathered + part
        return (gathered + turn(gathered, -1, 1)) * 0.125

    for i in range(4):
        chosen = index[4 * grp[0] + i]
        halves = []
        for c in range(4):
            first = jnp.broadcast_to(tables[chosen, c : c + 1, 0:128], (8, 128))
            second = jnp.broadcast_to(tables[chosen, c : c + 1, 128:256], (8, 128))
            last = lax.broadcasted_iota(jnp.int32, (8, 128), 1) == 127
            after_first = jnp.where(last, turn(second, -1, 1), turn(first, -1, 1))
            after_second = jnp.where(last, second, turn(second, -1, 1))
            halves.append((first, second, after_first - first, after_second - second))
        for m in range(4):
            density = coarse(lambda z, rows: density_of[0, z, rows, :], i, m)
            coord = 255.0 * jnp.clip((density - 0.9) / 0.6, 0.0, 1.0)
            cell = jnp.minimum(coord.astype(jnp.int32), 255)
            part = coord - cell.astype(f32)
            low_half = cell < 128
            entry = cell & 127

            def look(a, b):
                return jnp.where(
                    low_half,
                    jnp.take_along_axis(a, entry, axis=1),
                    jnp.take_along_axis(b, entry, axis=1),
                )

            for c, h in enumerate(halves):
                looked[i, m, c] = look(h[0], h[1]) + part * look(h[2], h[3])

    for copy in copies[2:]:
        copy.wait()

    def crossing(read):
        inverse = 1.0 / read(0)
        return read(2) * inverse, read(3) * inverse

    v_edge, w_edge = edge_pairs(crossing, *edges_of)
    for copy in copies[:2]:
        copy.wait()

    def depth(c, z, rows):
        total = None
        for k in range(4):
            addend = weights[k] * (uv[c, z + 5 + k, rows, :] - uv[c, z + 3 - k, rows, :])
            total = addend if k == 0 else total + addend
        return total

    for z in range(8):
        for b in range(4):
            rows = slice(16 * b, 16 * b + 16)
            chunk = 4 * z + b
            first = curls[0, z, rows, :] - depth(1, z, rows)
            second = depth(0, z, rows) - (curls[1, z, rows, :] + edge_tile(w_edge, chunk))
            third = curls[2, z, rows, :] + edge_tile(v_edge, chunk)
            spins[z, rows, :] = jnp.sqrt(first * first + second * second + third * third)

    lanes = lax.broadcasted_iota(jnp.int32, (8, 128), 1)
    rows_of = lax.broadcasted_iota(jnp.int32, (8, 128), 0)
    piece_lane = 16 * rows_of + 2 * (lanes & 7)
    outgoing = jnp.zeros((8, 128), f32)
    flipped = spread_flip(flip, lanes >> 1) == 1
    for i in range(4):
        total = None
        for m in range(4):
            spin = coarse(lambda z, rows: spins[z, rows, :], i, m)
            entries = [looked[i, m, c] for c in range(4)]
            opacity = opacity_gain * entries[3] * spin / (1.0 + spin) / ray_total
            piece = [entries[c] * opacity for c in range(3)] + [1.0 - opacity]
            total = piece if total is None else joined(total, piece, flipped)
        for span in (1, 2, 4):
            later = [turn(t, -span, 0) for t in total]
            total = joined(total, later, flipped)
        for c in range(4):
            row = jnp.broadcast_to(total[c][0:1, :], (8, 128))
            row = jnp.take_along_axis(row, piece_lane, axis=1)
            outgoing = jnp.where(lanes >> 3 == 4 * i + c, row, outgoing)
    for g in range(4):
        sent[8 * g : 8 * g + 8, :] = outgoing


def spread_flip(flip, lane):
    both = jnp.concatenate([flip[...], flip[...]], axis=1)
    return jnp.take_along_axis(jnp.broadcast_to(both, lane.shape), lane, axis=1)


def joined(near, far, flipped):
    colors = [
        jnp.where(flipped, far[c] + far[3] * near[c], near[c] + near[3] * far[c]) for c in range(3)
    ]
    return colors + [near[3] * far[3]]


def depth_kernel(partly, state, *refs):
    edges_of, out, fz = refs[:4], refs[4], refs[5]
    for z in range(8):
        for r in range(0, 64, 16):
            rows = slice(r, r + 16)
            rho, mx, my, mz, energy = (state[c, z, rows, :] for c in range(5))
            fields = up_fields(mz, energy, *primitives(rho, mx, my, mz, energy))
            for c in range(5):
                fz[c, z, rows, :] = fields[c]

    def packed(read):
        rho, mx, my, mz, energy = (read(c) for c in range(5))
        return east_fields(mx, my, mz, energy, *primitives(rho, mx, my, mz, energy))[:5]

    edges = edge_pairs(packed, *edges_of)
    for c in range(5):
        for z in range(8):
            for b in range(4):
                rows = slice(16 * b, 16 * b + 16)
                total = edge_tile(edges[c], 4 * z + b)
                for k in range(4):
                    if z + k + 1 < 8:
                        total = total + weights[k] * fz[c, z + k + 1, rows, :]
                    if z - k - 1 >= 0:
                        total = total - weights[k] * fz[c, z - k - 1, rows, :]
                out[c, z, rows, :] = partly[c, z, rows, :] - step_size * total


def last_kernel(partly, *refs):
    below_in, below_b, above_in, above_b, out, fz, held, below_a, above_a, sems, out_sems = refs
    copies = [
        pltpu.make_async_copy(below_in, below_a, sems.at[0]),
        pltpu.make_async_copy(above_in, above_a, sems.at[1]),
    ]
    for copy in copies:
        copy.start()

    def sending(c):
        return pltpu.make_async_copy(held.at[c], out.at[c], out_sems.at[c])

    for side, (a, b) in enumerate(((below_a, below_b), (above_a, above_b))):
        copies[side].wait()
        for p in range(4):
            for r in range(0, 64, 16):
                rows = slice(r, r + 16)
                u, v = a[0, p, rows, :], a[1, p, rows, :]
                rho, mz, energy = b[0, p, rows, :], b[1, p, rows, :], b[2, p, rows, :]
                w = mz / rho
                pressure = gamma_less * (energy - 0.5 * (rho * (u * u + v * v) + mz * w))
                fields = up_fields(mz, energy, u, v, w, pressure)
                for c in range(5):
                    fz[c, 4 * side + p, rows, :] = step_size * fields[c]
    for c in range(5):
        for z in range(8):
            for r in range(0, 64, 16):
                rows = slice(r, r + 16)
                total = partly[c, z, rows, :]
                for k in range(4):
                    if z + k + 1 >= 8:
                        total = total - weights[k] * fz[c, 4 + z + k + 1 - 8, rows, :]
                    if z - k - 1 < 0:
                        total = total + weights[k] * fz[c, z - k - 1 + 4, rows, :]
                held[c, z, rows, :] = total
        sending(c).start()
    for c in range(5):
        sending(c).wait()


def compose_kernel(me, depth, owner, flip, pieces, out):
    lane = lax.broadcasted_iota(jnp.int32, (4, 128), 1)
    channel = lane >> 3 & 3
    lanes = lax.broadcasted_iota(jnp.int32, (8, 128), 1)
    flipped = spread_flip(flip, 8 * depth[0] + (lanes & 7))[0:4] == 1

    def passing(x):
        return jnp.where(
            channel == 3,
            x,
            jnp.where(
                channel == 2, turn(x, -8, 1), jnp.where(channel == 1, turn(x, -16, 1), turn(x, -24, 1))
            ),
        )

    total = pieces[:, 0, :]
    total_pass = passing(total)
    for j in range(1, 8):
        later = pieces[:, j, :]
        later_pass = passing(later)
        both = total_pass * later_pass
        color = jnp.where(flipped, later + later_pass * total, total + total_pass * later)
        total = jnp.where(channel == 3, both, color)
        total_pass = both
    total = jnp.where(channel == 3, 1.0 - total, total)
    sub = lax.broadcasted_iota(jnp.int32, (8, 128), 0)
    result = jnp.zeros((8, 128), f32)
    count = jnp.int32(0)
    shifted = [turn(total, -32 * i, 1) for i in range(4)]
    for b in range(16):
        mine = owner[b] == me[0]
        slot = jnp.where(mine, count, -1)
        count = jnp.where(mine, count + 1, count)
        row = jnp.broadcast_to(shifted[b % 4][b // 4 : b // 4 + 1, :], (8, 128))
        result = jnp.where(sub == slot, row, result)
    for c in range(4):
        out[:, c, :] = turn(result, -8 * c, 1)[:, 0:8]


def shape(*dims):
    return jax.ShapeDtypeStruct(dims, f32)


def ring(axis, step):
    count = lax.axis_size(axis)
    return [(i, (i + step) % count) for i in range(count)]


def after(value, *others):
    return lax.optimization_barrier((value, *others))[0]


def local(state, tf_table, owner, tf_index, view_flip):
    grp = lax.axis_index("grp")
    gy = lax.axis_index("gy")
    groups, depth = lax.axis_size("grp"), lax.axis_size("gy")
    low_a, high_a = pl.pallas_call(
        first_pack_kernel,
        out_shape=(shape(2, 4, 64, 128), shape(2, 4, 64, 128)),
        in_specs=[HB],
        out_specs=(VM, VM),
        scratch_shapes=[pltpu.VMEM((3, 8, 64, 128), f32), pltpu.SemaphoreType.DMA((6,))],
        compiler_params=params(),
    )(in_hbm(state))
    y_low, y_high = pl.pallas_call(
        row_pack_kernel,
        out_shape=(shape(5, 4, 8, 128), shape(5, 4, 8, 128)),
        in_specs=[VM],
        out_specs=(VM, VM),
        compiler_params=params(),
    )(after(state, low_a))
    from_below_a = lax.ppermute(high_a, "grp", ring("grp", 1))
    from_above_a = lax.ppermute(low_a, "grp", ring("grp", -1))
    from_south = lax.ppermute(y_high, "gy", ring("gy", 1))
    from_north = lax.ppermute(y_low, "gy", ring("gy", -1))
    x_low, x_high = pl.pallas_call(
        second_pack_kernel,
        out_shape=(shape(5, 16, 128), shape(5, 16, 128)),
        in_specs=[VM],
        out_specs=(VM, VM),
        compiler_params=params(),
    )(after(state, y_low))
    from_left = lax.ppermute(x_high, "gx", ring("gx", 1))
    from_right = lax.ppermute(x_low, "gx", ring("gx", -1))
    partly, curls = pl.pallas_call(
        inner_kernel,
        out_shape=(shape(5, 8, 64, 128), shape(3, 8, 64, 128)),
        in_specs=[VM, VM, VM],
        out_specs=(VM, VM),
        scratch_shapes=[
            pltpu.VMEM((256, 256), jnp.bfloat16),
            pltpu.VMEM((7, 8, 80, 128), f32),
            pltpu.VMEM((7, 64, 256), jnp.bfloat16),
            pltpu.VMEM((7, 64, 128), f32),
        ],
        compiler_params=params(12),
        cost_estimate=weight(0.3),
    )(state, from_south, from_north)

    low_b, high_b = pl.pallas_call(
        third_pack_kernel,
        out_shape=(shape(3, 4, 64, 128), shape(3, 4, 64, 128)),
        in_specs=[VM],
        out_specs=(VM, VM),
        compiler_params=params(),
        cost_estimate=weight(0.3),
    )(after(state, x_low))
    low_b, high_b = lax.optimization_barrier((low_b, high_b, from_above_a, from_below_a))[:2]
    from_above_b = lax.ppermute(low_b, "grp", ring("grp", -1))
    from_below_b = lax.ppermute(high_b, "grp", ring("grp", 1))

    flip = view_flip[None, :]
    sent = pl.pallas_call(
        functools.partial(render_kernel, float(depth * 32)),
        out_shape=shape(32, 128),
        in_specs=[SM] * 2 + [VM] * 5 + [HB] * 4 + [VM],
        out_specs=VM,
        scratch_shapes=[
            pltpu.VMEM((8, 64, 128), f32),
            pltpu.VMEM((2, 16, 64, 128), f32),
            pltpu.VMEM((4, 4, 4, 8, 128), f32),
            pltpu.VMEM((5, 16, 128), f32),
            pltpu.VMEM((5, 16, 128), f32),
            pltpu.SemaphoreType.DMA((4,)),
        ],
        compiler_params=params(4),
        cost_estimate=weight(60),
    )(
        grp[None], tf_index, flip, state, curls,
        x_low, x_high, from_left, from_right, in_hbm(from_below_a), in_hbm(from_above_a), tf_table,
    )
    received = lax.all_to_all(sent, ("grp", "gy"), 0, 0, tiled=True).reshape(groups, depth, 128)
    most = pl.pallas_call(
        depth_kernel,
        out_shape=shape(5, 8, 64, 128),
        in_specs=[VM] * 6,
        out_specs=VM,
        scratch_shapes=[pltpu.VMEM((5, 8, 64, 128), f32)],
        compiler_params=params(6),
    )(after(partly, sent), state, x_low, x_high, from_left, from_right)
    new_state = pl.pallas_call(
        last_kernel,
        out_shape=shape(5, 8, 64, 128),
        in_specs=[VM, HB, VM, HB, VM],
        out_specs=HB,
        scratch_shapes=[
            pltpu.VMEM((5, 8, 64, 128), f32),
            pltpu.VMEM((5, 8, 64, 128), f32),
            pltpu.VMEM((2, 4, 64, 128), f32),
            pltpu.VMEM((2, 4, 64, 128), f32),
            pltpu.SemaphoreType.DMA((2,)),
            pltpu.SemaphoreType.DMA((5,)),
        ],
        compiler_params=params(6),
    )(most, in_hbm(from_below_a), from_below_b, in_hbm(from_above_a), from_above_b)
    image = pl.pallas_call(
        compose_kernel,
        out_shape=shape(8, 4, 8),
        in_specs=[SM, SM, SM, VM, VM],
        out_specs=VM,
        compiler_params=params(),
    )(grp[None], gy[None], owner[:, 0], flip, after(received, new_state))
    return (new_state, image)


def solution(mesh):
    placed = (P(None, "grp", "gy", "gx"), P(), P(), P(), P("gx"))
    return jax.shard_map(
        local,
        mesh=mesh,
        in_specs=placed,
        out_specs=(P(None, "grp", "gy", "gx"), P("grp", None, ("gx", "gy"))),
        check_vma=False,
    )
```
